32 devices in a mesh: seq: 8 (over z, y), head: 4 (over x, core).
Axes of the slice: x: 2, y: 2, z: 4, core: 2. Of those that a mesh axis runs over, the one named last changes fastest.
Arguments:
- queries: bfloat16 [32768, 2048], P('seq', 'head'), may hold values from -6 to 6
- keys: bfloat16 [32768, 2048], P('seq', 'head'), may hold values from -0.59765625 to 0.59765625
- values: bfloat16 [32768, 2048], P('seq', 'head'), may hold values from -6 to 6
- norm_gain: float32 [2048], replicated, may hold values from 0.1 to 1.9
Outputs:
- normed: bfloat16 [32768, 2048], P(('seq', 'head'))
The draws below stay inside these ranges and needn't reach their ends.
All inputs are finite; a program needn't handle non-finite values.
Results may differ from the reference program's by a relative error of at most 0.0058.
Values may be sent and summed in bfloat16 or wider, within the bound.
No kernel may reach another device: no remote copies, remote signals or barrier semaphores. Data moves between devices by JAX's collectives and lax.ppermute only.
A program may use at most 128 MiB of HBM per device.

```python
import jax
import jax.numpy as jnp
from jax import lax

DH = 128
H = 16
BLK = 512
TOKENS = 32768
F = 2048


def steps_of(stream_key, dims, split, smallest, largest):
    def one(dim, shards_of):
        steps = jax.random.uniform(jax.random.fold_in(jax.random.fold_in(stream_key, 6), dim), (shards_of,), jnp.float32, smallest / len(split), largest / len(split))
        return jnp.repeat(jnp.exp(steps), dims[dim] // shards_of).reshape((-1,) + (1,) * (len(dims) - dim - 1))

    gain = one(*split[0])
    for cut in split[1:]:
        gain = gain * one(*cut)
    return gain


def noise(rng, dims, spread, bound, shards=(), kind=jnp.bfloat16):
    entries = jax.random.normal(rng, dims, jnp.float32) * spread
    if len(shards) > 0:
        entries = steps_of(rng, dims, shards, -0.22, 0.18) * entries
    return jnp.clip(entries, min=-bound, max=bound).astype(kind)


def setup_inputs(seed: int = 0) -> dict:
    seeds = jax.random.split(jax.random.key(seed), 5)
    queries = noise(seeds[0], (TOKENS, F), 1.0, 6.0, ((0, 8), (1, 4)))
    keys = noise(seeds[1], (TOKENS, F), 0.088, 0.59765625, ((0, 8), (1, 4)))
    values = noise(seeds[2], (TOKENS, F), 1.0, 6.0, ((0, 8), (1, 4)))
    norm_gain = jnp.clip(1.0 + 0.18 * jax.random.normal(seeds[3], (F,), jnp.float32), 0.1, 1.9)
    return {"queries": queries, "keys": keys, "values": values, "norm_gain": norm_gain}


def reference(queries, keys, values, norm_gain):
    blocks = TOKENS // BLK

    def split_heads(array):
        return array.reshape(blocks, BLK, H, DH).transpose(2, 0, 1, 3)

    def one_head(operands):
        query_rows, key_rows, value_rows = operands
        query_rows = query_rows.astype(jnp.float32)
        key_rows = key_rows.astype(jnp.float32)
        value_rows = value_rows.astype(jnp.float32)
        block_state = jnp.einsum('nbd,nbe->nde', key_rows, value_rows, precision=lax.Precision.HIGHEST)
        running = jnp.cumsum(block_state, axis=0)
        prefix = jnp.concatenate([jnp.zeros((1, DH, DH), jnp.float32), running[:-1]], axis=0)
        prefix_low = prefix.astype(jnp.bfloat16).astype(jnp.float32)
        inter = jnp.einsum('nbd,nde->nbe', query_rows, prefix_low, precision=lax.Precision.HIGHEST)
        scores = jnp.einsum('nbd,ncd->nbc', query_rows, key_rows, precision=lax.Precision.HIGHEST)
        causal = jnp.arange(BLK)[:, None] >= jnp.arange(BLK)[None, :]
        scores = jnp.where(causal[None], scores, jnp.zeros_like(scores))
        scores = scores.astype(jnp.bfloat16).astype(jnp.float32)
        intra = jnp.einsum('nbc,nce->nbe', scores, value_rows, precision=lax.Precision.HIGHEST)
        return (inter + intra).astype(jnp.bfloat16)
    attention = lax.map(one_head, (split_heads(queries), split_heads(keys), split_heads(values)))
    attention = attention.transpose(1, 2, 0, 3).reshape(TOKENS, F)
    widened = attention.astype(jnp.float32)
    meansq = lax.optimization_barrier(jnp.mean(widened * widened, axis=-1, keepdims=True))
    return (widened * lax.rsqrt(meansq + 1e-06) * norm_gain[None, :]).astype(jnp.bfloat16)
```

```python
import jax
import jax.numpy as jnp
from jax import lax
from jax.experimental import pallas as pl
from jax.experimental.pallas import tpu as pltpu
from jax.sharding import PartitionSpec as P

DH = 128
BLK = 512
HALF = 256
EPS = 1e-06
VMEM = 48 * 1024 * 1024


def params():
    return pltpu.CompilerParams(vmem_limit_bytes=VMEM)


def state_kernel(k_ref, v_ref, within_ref, total_ref, acc):
    step = pl.program_id(0)

    @pl.when(step == 0)
    def _():
        acc[...] = jnp.zeros_like(acc)

    heads = acc.shape[0]
    for h in range(heads):
        cols = pl.ds(h * DH, DH)
        within_ref[0, h] = acc[h]
        acc[h] += lax.dot_general(
            k_ref[:, cols], v_ref[:, cols], (((0,), (0,)), ((), ())),
            preferred_element_type=jnp.float32,
        )

    @pl.when(step == pl.num_programs(0) - 1)
    def _():
        total_ref[...] = acc[...].astype(jnp.bfloat16)


def block_states(keys, values):
    rows, width = keys.shape
    heads, blocks = width // DH, rows // BLK
    block = pl.BlockSpec((BLK, width), lambda n: (n, 0))
    return pl.pallas_call(
        state_kernel,
        grid=(blocks,),
        in_specs=[block, block],
        out_specs=[
            pl.BlockSpec((1, heads, DH, DH), lambda n: (n, 0, 0, 0)),
            pl.BlockSpec((heads, DH, DH), lambda n: (0, 0, 0)),
        ],
        out_shape=[
            jax.ShapeDtypeStruct((blocks, heads, DH, DH), jnp.float32),
            jax.ShapeDtypeStruct((heads, DH, DH), jnp.bfloat16),
        ],
        scratch_shapes=[pltpu.VMEM((heads, DH, DH), jnp.float32)],
        compiler_params=params(),
        cost_estimate=pl.CostEstimate(
            flops=4 * rows * width * DH, bytes_accessed=4 * rows * width, transcendentals=0
        ),
        name="block_states",
    )(keys, values)


def attention_kernel(first, count, with_before, quarter_ref, q_ref, k_ref, v_ref, within_ref, *rest):
    if with_before:
        before_ref, out_ref = rest
        state = (within_ref[0, 0] + before_ref[0]).astype(jnp.bfloat16)
    else:
        (out_ref,) = rest
        state = within_ref[0, 0].astype(jnp.bfloat16)
    row = lax.broadcasted_iota(jnp.int32, (HALF, HALF), 0)
    col = lax.broadcasted_iota(jnp.int32, (HALF, HALF), 1)
    for i in range(count):
        here = pl.ds(i * HALF, HALF)
        q = q_ref[here, :]
        out = jnp.dot(q, state, preferred_element_type=jnp.float32)
        for j in range(first + i + 1):
            there = pl.ds(j * HALF, HALF)
            scores = lax.dot_general(
                q, k_ref[there, :], (((1,), (1,)), ((), ())), preferred_element_type=jnp.float32
            )
            if j == first + i:
                scores = jnp.where(row >= col, scores, 0.0)
            out += jnp.dot(
                scores.astype(jnp.bfloat16), v_ref[there, :], preferred_element_type=jnp.float32
            )
        out_ref[here, :] = out.astype(jnp.bfloat16)


def attention_rows(queries, keys, values, within, before, quarter, start, size, head, heads):
    rows, width = queries.shape
    share = rows // 4
    halves = min(size, BLK) // HALF
    first = (start % BLK) // HALF
    steps = size // (halves * HALF)
    whole = (steps, heads)
    q_block = halves * HALF
    q_base, q_quarter = start // q_block, share // q_block
    k_base, k_quarter = start // BLK, share // BLK
    k_rows = BLK if first + halves > 1 else HALF
    k_scale = BLK // k_rows
    in_specs = [
        pl.BlockSpec((q_block, DH), lambda n, h, s: (s[0] * q_quarter + q_base + n, head + h)),
        pl.BlockSpec((k_rows, DH), lambda n, h, s: ((s[0] * k_quarter + k_base + n) * k_scale, head + h)),
        pl.BlockSpec((k_rows, DH), lambda n, h, s: ((s[0] * k_quarter + k_base + n) * k_scale, head + h)),
        pl.BlockSpec((1, 1, DH, DH), lambda n, h, s: (s[0] * k_quarter + k_base + n, head + h, 0, 0)),
    ]
    operands = [queries, keys, values, within]
    if before is not None:
        in_specs.append(pl.BlockSpec((1, DH, DH), lambda n, h, s: (head + h, 0, 0)))
        operands.append(before)

    def kernel(*refs):
        attention_kernel(first, halves, before is not None, *refs)

    return pl.pallas_call(
        kernel,
        grid_spec=pltpu.PrefetchScalarGridSpec(
            num_scalar_prefetch=1,
            grid=whole,
            in_specs=in_specs,
            out_specs=pl.BlockSpec((q_block, DH), lambda n, h, s: (n, h)),
        ),
        out_shape=jax.ShapeDtypeStruct((size, heads * DH), jnp.bfloat16),
        compiler_params=params(),
        cost_estimate=pl.CostEstimate(
            flops=4 * size * heads * DH * BLK, bytes_accessed=8 * size * heads * DH, transcendentals=0
        ),
        name="attention_rows",
    )(quarter, *operands)


def norm_kernel(head_ref, gain_ref, own_ref, mate_ref, x2_ref, x3_ref, l2_ref, l3_ref, q2_ref, q3_ref,
                b2_ref, b3_ref, *rest):
    out_ref = rest[-1]
    head = head_ref[0]
    width = own_ref.shape[1]
    early = l2_ref.shape[1]
    pieces = [(own_ref[...], 0, 0), (mate_ref[...], 1, 0)]
    for partner, x_ref, l_ref, q_ref, b_ref in ((2, x2_ref, l2_ref, q2_ref, b2_ref), (3, x3_ref, l3_ref, q3_ref, b3_ref)):
        late = l_ref[...].astype(jnp.float32) + jnp.dot(
            q_ref[...], b_ref[...], preferred_element_type=jnp.float32
        )
        pieces.append((late.astype(jnp.bfloat16), partner, 0))
        pieces.append((x_ref[...], partner, early))
    total = 0.0
    for piece, _, _ in pieces:
        wide = piece.astype(jnp.float32)
        total += jnp.sum(wide * wide, axis=-1, keepdims=True)
    scale = lax.rsqrt(total / (4 * width) + EPS)
    for piece, partner, offset in pieces:
        at = pl.multiple_of((head ^ partner) * width + offset, DH)
        cols = pl.ds(at, piece.shape[1])
        out_ref[:, cols] = (piece.astype(jnp.float32) * scale * gain_ref[:, cols]).astype(jnp.bfloat16)


def norm_rows(head, gain, own, mate, x2, x3, l2, l3, q2, q3, b2, b3, start, size, out):
    share, width = own.shape
    tile = min(size, 256)
    base = start // tile
    whole = pl.BlockSpec((tile, width), lambda n, s: (base + n, 0))
    main = pl.BlockSpec((tile, x2.shape[1]), lambda n, s: (n, 0))
    early = pl.BlockSpec((tile, DH), lambda n, s: (base + n, 0))
    state = pl.BlockSpec((DH, DH), lambda n, s: (0, 0))
    in_specs = [
        pl.BlockSpec((1, 4 * width), lambda n, s: (0, 0)),
        whole, whole, main, main, early, early, early, early, state, state,
    ]
    operands = [gain, own, mate, x2, x3, l2, l3, q2, q3, b2, b3]
    aliases = {}
    if out is not None:
        in_specs.append(pl.BlockSpec(memory_space=pl.ANY))
        operands.append(out)
        aliases = {len(operands): 0}
    return pl.pallas_call(
        norm_kernel,
        grid_spec=pltpu.PrefetchScalarGridSpec(
            num_scalar_prefetch=1,
            grid=(size // tile,),
            in_specs=in_specs,
            out_specs=pl.BlockSpec((tile, 4 * width), lambda n, s: (base + n, 0)),
        ),
        out_shape=jax.ShapeDtypeStruct((share, 4 * width), jnp.bfloat16),
        input_output_aliases=aliases,
        compiler_params=params(),
        cost_estimate=pl.CostEstimate(
            flops=16 * size * width, bytes_accessed=16 * size * width, transcendentals=size
        ),
        name="norm_rows",
    )(head, *operands)


def swap(x, axis, size, bit):
    return lax.ppermute(x, axis, [(i, i ^ bit) for i in range(size)])


def sums_before(total, size):
    mine = lax.axis_index("seq")
    group = total.astype(jnp.float32)
    before = jnp.zeros_like(group)
    bit = 1
    if size % 4 == 0:
        got = [swap(total, "seq", size, k).astype(jnp.float32) for k in (1, 2, 3)]
        for k, piece in zip((1, 2, 3), got):
            before += jnp.where((mine ^ k) < mine, piece, 0.0)
            group += piece
        bit = 4
    while bit < size:
        piece = swap(group.astype(jnp.bfloat16), "seq", size, bit).astype(jnp.float32)
        before += jnp.where((mine & bit) > 0, piece, 0.0)
        group += piece
        bit *= 2
    return before


CHUNKS = ((0, 512), (512, 256), (768, 256))


def shards(seq_size, queries, keys, values, norm_gain):
    rows, width = queries.shape
    heads = width // DH
    share = rows // 4
    head = lax.axis_index("head")
    quarter = [jnp.full((1,), head ^ k, jnp.int32) for k in range(4)]

    early_q = [
        swap(lax.dynamic_slice(queries, ((head ^ k) * share, 0), (share, DH)), "head", 4, k) for k in (2, 3)
    ]
    within, total = block_states(keys, values)
    early_l = [
        swap(attention_rows(queries, keys, values, within, None, quarter[k], 0, share, 0, 1), "head", 4, k)
        for k in (2, 3)
    ]
    before = sums_before(total, seq_size)
    before_low = before[0].astype(jnp.bfloat16)
    early_b = [swap(before_low, "head", 4, k) for k in (2, 3)]
    main = []
    for start, size in CHUNKS:
        main.append([
            swap(
                attention_rows(queries, keys, values, within, before, quarter[k], start, size, 1, heads - 1),
                "head", 4, k,
            )
            for k in (2, 3)
        ])
    mate = swap(attention_rows(queries, keys, values, within, before, quarter[1], 0, share, 0, heads), "head", 4, 1)
    own = attention_rows(queries, keys, values, within, before, quarter[0], 0, share, 0, heads)
    gain = norm_gain.reshape(1, -1)
    out = None
    for (start, size), (x2, x3) in zip(CHUNKS, main):
        out = norm_rows(
            quarter[0], gain, own, mate, x2, x3, early_l[0], early_l[1], early_q[0], early_q[1],
            early_b[0], early_b[1], start, size, out,
        )
    return out


def solution(mesh):
    seq_size = mesh.shape["seq"]

    def body(queries, keys, values, norm_gain):
        return shards(seq_size, queries, keys, values, norm_gain)

    return jax.shard_map(
        body,
        mesh=mesh,
        in_specs=(P("seq", "head"), P("seq", "head"), P("seq", "head"), P()),
        out_specs=P(("seq", "head"), None),
        check_vma=False,
    )
```

```python
import functools

import jax
import jax.numpy as jnp
from jax import lax
from jax.experimental import pallas as pl
from jax.experimental.pallas import tpu as pltpu
from jax.sharding import PartitionSpec as P

DH = 128
BLK = 512
HALF = 256
EXTRA = 48
EPS = 1e-06
COST = pl.CostEstimate(flops=1024, bytes_accessed=1024, transcendentals=0)
LONG = pl.CostEstimate(flops=10**12, bytes_accessed=1024, transcendentals=0)


def params(mib=50):
    return pltpu.CompilerParams(vmem_limit_bytes=mib * 1024 * 1024)


def state_kernel(parts, tokens, head_ref, k_ref, v_ref, q2_ref, q3_ref, *rest):
    within_ref, total_ref, *rest = rest[tokens:]
    outs, (k_buf, v_buf, k_sem, v_sem) = rest[:-4], rest[-4:]
    rows, width = k_buf.shape
    heads, part, share = width // DH, rows // parts, rows // 4
    copies = []
    for p in range(parts):
        at = pl.ds(p * part, part)
        pair = (
            pltpu.make_async_copy(k_ref.at[at], k_buf.at[at], k_sem.at[p]),
            pltpu.make_async_copy(v_ref.at[at], v_buf.at[at], v_sem.at[p]),
        )
        for copy in pair:
            copy.start()
        copies.append(pair)
    acc = [jnp.zeros((DH, DH), jnp.float32) for _ in range(heads)]
    for p in range(parts):
        for copy in copies[p]:
            copy.wait()
        for n in range(p * part // BLK, (p + 1) * part // BLK):
            at = pl.ds(n * BLK, BLK)
            for h in range(heads):
                cols = pl.ds(h * DH, DH)
                within_ref[n, h] = acc[h]
                acc[h] = acc[h] + lax.dot_general(
                    k_buf[at, cols], v_buf[at, cols], (((0,), (0,)), ((), ())),
                    preferred_element_type=jnp.float32,
                )
    for h in range(heads):
        total_ref[h] = acc[h].astype(jnp.bfloat16)
    blocks = share // BLK
    cols = pl.ds(width - DH, DH)
    for side, q_ref in ((2, q2_ref), (3, q3_ref)):
        for n in range(blocks):
            block = (head_ref[0] ^ side) * blocks + n
            at = pl.ds(pl.multiple_of(block * BLK, BLK), BLK)
            attend(
                0, BLK // HALF, 1, q_ref.at[pl.ds(n * BLK, BLK)], k_buf.at[at, cols], v_buf.at[at, cols],
                within_ref.at[pl.ds(block, 1), pl.ds(heads - 1, 1)], None, outs[(side - 2) * blocks + n],
            )


def block_states(head, keys, values, slices, *tokens):
    rows, width = keys.shape
    heads, blocks = width // DH, rows // BLK
    parts = 4 if blocks % 4 == 0 else 1
    anywhere = pl.BlockSpec(memory_space=pl.ANY)
    vmem = pl.BlockSpec(memory_space=pltpu.VMEM)
    pieces = 2 * (blocks // 4)
    return pl.pallas_call(
        functools.partial(state_kernel, parts, len(tokens)),
        in_specs=[pl.BlockSpec(memory_space=pltpu.SMEM), anywhere, anywhere, vmem, vmem] + [anywhere] * len(tokens),
        out_specs=[vmem] * (2 + pieces),
        out_shape=[
            jax.ShapeDtypeStruct((blocks, heads, DH, DH), jnp.float32),
            jax.ShapeDtypeStruct((heads, DH, DH), jnp.bfloat16),
        ] + [jax.ShapeDtypeStruct((BLK, DH), jnp.bfloat16)] * pieces,
        scratch_shapes=[
            pltpu.VMEM((rows, width), jnp.bfloat16),
            pltpu.VMEM((rows, width), jnp.bfloat16),
            pltpu.SemaphoreType.DMA((parts,)),
            pltpu.SemaphoreType.DMA((parts,)),
        ],
        compiler_params=params(62),
        cost_estimate=COST,
        name="block_states",
    )(head, keys, values, *slices, *tokens)


def attend(first, halves, heads, q_ref, k_ref, v_ref, within_ref, before_ref, out_ref):
    row = lax.broadcasted_iota(jnp.int32, (HALF, HALF), 0)
    col = lax.broadcasted_iota(jnp.int32, (HALF, HALF), 1)
    for h in range(heads):
        cols = pl.ds(h * DH, DH)
        state = within_ref[0, h]
        if before_ref is not None:
            state = state + before_ref[h]
        q = q_ref[:, cols]
        out = jnp.dot(q, state.astype(jnp.bfloat16), preferred_element_type=jnp.float32)
        outs = [out[i * HALF:(i + 1) * HALF] for i in range(halves)]
        for j in range(first + halves):
            start = max(j - first, 0)
            there = pl.ds(j * HALF, HALF)
            scores = lax.dot_general(
                q[start * HALF:], k_ref[there, cols], (((1,), (1,)), ((), ())),
                preferred_element_type=jnp.float32,
            )
            low = []
            for i in range(start, halves):
                piece = scores[(i - start) * HALF:(i - start + 1) * HALF]
                if first + i == j:
                    piece = jnp.where(row >= col, piece, 0.0)
                low.append(piece.astype(jnp.bfloat16))
            low = jnp.concatenate(low, axis=0) if len(low) > 1 else low[0]
            more = jnp.dot(low, v_ref[there, cols], preferred_element_type=jnp.float32)
            for i in range(start, halves):
                outs[i] = outs[i] + more[(i - start) * HALF:(i - start + 1) * HALF]
        for i in range(halves):
            out_ref[pl.ds(i * HALF, HALF), cols] = outs[i].astype(out_ref.dtype)


def attention_rows(arrays, before, at, sides, start, size, head, heads, kind, tokens, cost=None):
    queries, keys, values, within = arrays
    rows, width = queries.shape
    share = rows // 4
    halves = size // HALF
    first = (start % BLK) // HALF
    k_rows = BLK if first + halves > 1 else HALF
    span = heads * DH
    across = head // heads
    count = len(sides)

    def quarter(n, s):
        side = sides[0]
        for i in range(1, count):
            side = jnp.where(n == i, sides[i], side)
        return s[0] ^ side

    def block(n, s):
        return quarter(n, s) * (share // BLK) + start // BLK

    keys_spec = pl.BlockSpec((k_rows, span), lambda n, s: (block(n, s) * (BLK // k_rows), across))
    in_specs = [
        pl.BlockSpec((size, span), lambda n, s: (quarter(n, s) * (share // size) + start // size, across)),
        keys_spec,
        keys_spec,
        pl.BlockSpec((1, heads, DH, DH), lambda n, s: (block(n, s), across, 0, 0)),
    ]
    operands = [queries, keys, values, within]
    if before is not None:
        in_specs.append(pl.BlockSpec(before.shape, lambda n, s: (0, 0, 0)))
        operands.append(before)
    in_specs += [pl.BlockSpec(memory_space=pl.ANY)] * len(tokens)

    def kernel(ids_ref, q_ref, k_ref, v_ref, within_ref, *rest):
        before_ref = None if before is None else rest[0]
        outs = rest[len(rest) - count:]
        for n in range(count):
            @pl.when(pl.program_id(0) == n)
            def _(n=n):
                attend(first, halves, heads, q_ref, k_ref, v_ref, within_ref, before_ref, outs[n])

    return pl.pallas_call(
        kernel,
        grid_spec=pltpu.PrefetchScalarGridSpec(
            num_scalar_prefetch=1,
            grid=(count,),
            in_specs=in_specs,
            out_specs=[pl.BlockSpec((size, span), lambda n, s: (0, 0))] * count,
        ),
        out_shape=[jax.ShapeDtypeStruct((size, span), kind)] * count,
        compiler_params=params(),
        cost_estimate=COST if cost is None else cost,
        name="attention_rows",
    )(at, *operands, *tokens)


def attention_quarter(arrays, before, at, side, kind, tokens):
    queries, keys, values, within = arrays
    rows, width = queries.shape
    share = rows // 4
    heads, blocks = width // DH, share // BLK
    block = pl.BlockSpec((BLK, width), lambda n, s: ((s[0] ^ side) * blocks + n, 0))
    state = pl.BlockSpec((1, heads, DH, DH), lambda n, s: ((s[0] ^ side) * blocks + n, 0, 0, 0))
    in_specs = [block, block, block, state]
    operands = [queries, keys, values, within]
    if before is not None:
        in_specs.append(pl.BlockSpec(before.shape, lambda n, s: (0, 0, 0)))
        operands.append(before)
    in_specs += [pl.BlockSpec(memory_space=pl.ANY)] * len(tokens)

    def kernel(quarter_ref, q_ref, k_ref, v_ref, within_ref, *rest):
        before_ref = None if before is None else rest[0]
        attend(0, BLK // HALF, heads, q_ref, k_ref, v_ref, within_ref, before_ref, rest[-1])

    return pl.pallas_call(
        kernel,
        grid_spec=pltpu.PrefetchScalarGridSpec(
            num_scalar_prefetch=1,
            grid=(blocks,),
            in_specs=in_specs,
            out_specs=pl.BlockSpec((BLK, width), lambda n, s: (n, 0)),
        ),
        out_shape=jax.ShapeDtypeStruct((share, width), kind),
        compiler_params=params(),
        cost_estimate=COST,
        name="attention_quarter",
    )(at, *operands, *tokens)


def late_kernel(count, heads, embed, ids_ref, *refs):
    before_ref = refs[2 * count]
    outs = refs[len(refs) - count:]
    for n in range(count):
        q_ref, local_ref, out_ref = refs[2 * n], refs[2 * n + 1], outs[n]
        size = q_ref.shape[0]
        for h in range(heads):
            cols = pl.ds(h * DH, DH)
            out = local_ref[:, cols] + jnp.dot(
                q_ref[:, cols], before_ref[h].astype(jnp.bfloat16), preferred_element_type=jnp.float32
            )
            out_ref[pl.ds(0, size), cols] = out.astype(jnp.bfloat16)
        if embed:
            low = before_ref[heads].astype(jnp.bfloat16)
            for c in range(heads):
                high = min((c + 1) * EXTRA, DH)
                out_ref[pl.ds(size, high - c * EXTRA), pl.ds(c * DH, DH)] = low[c * EXTRA:high]


def late_rows(queries, before, at, sides, locals_, heads, embed, tokens):
    count = len(sides)
    size, span = locals_[0].shape
    steps = 1 if embed else size // BLK
    rows = size // steps
    share = queries.shape[0] // 4
    in_specs, operands = [], []
    for n in range(count):
        in_specs.append(pl.BlockSpec((rows, span), lambda i, s, side=sides[n]: ((s[0] ^ side) * (share // rows) + i, 0)))
        in_specs.append(pl.BlockSpec((rows, span), lambda i, s: (i, 0)))
        operands += [queries, locals_[n]]
    in_specs.append(pl.BlockSpec(before.shape, lambda i, s: (0, 0, 0)))
    in_specs += [pl.BlockSpec(memory_space=pl.ANY)] * len(tokens)
    more = EXTRA if embed else 0
    return pl.pallas_call(
        functools.partial(late_kernel, count, heads, embed),
        grid_spec=pltpu.PrefetchScalarGridSpec(
            num_scalar_prefetch=1,
            grid=(steps,),
            in_specs=in_specs,
            out_specs=[pl.BlockSpec((rows + more, span), lambda i, s: (i, 0))] * count,
        ),
        out_shape=[jax.ShapeDtypeStruct((size + more, span), jnp.bfloat16)] * count,
        compiler_params=params(),
        cost_estimate=COST,
        name="late_rows",
    )(at, *operands, before, *tokens)


def norm_kernel(head_ref, gain_ref, own_ref, mate_ref, x2_ref, x3_ref, l2_ref, l3_ref, q2_ref, q3_ref,
                b2_ref, b3_ref, *rest):
    out_ref = rest[-1]
    head = head_ref[0]
    tile, width = own_ref.shape
    pieces = [(own_ref[...], 0, 0), (mate_ref[...], 1, 0)]
    sides = ((2, x2_ref, l2_ref, q2_ref, b2_ref), (3, x3_ref, l3_ref, q3_ref, b3_ref))
    for partner, x_ref, l_ref, q_ref, b_ref in sides:
        base = b_ref.shape[0] - EXTRA
        parts = []
        for c in range(b_ref.shape[1] // DH):
            high = min((c + 1) * EXTRA, DH)
            parts.append(b_ref[pl.ds(base, high - c * EXTRA), pl.ds(c * DH, DH)])
        state = jnp.concatenate(parts, axis=0)
        late = l_ref[...].astype(jnp.float32) + jnp.dot(q_ref[...], state, preferred_element_type=jnp.float32)
        pieces.append((x_ref[...], partner, 0))
        pieces.append((late.astype(jnp.bfloat16), partner, width - DH))
    total = 0.0
    for piece, _, _ in pieces:
        wide = piece.astype(jnp.float32)
        total += jnp.sum(wide * wide, axis=-1, keepdims=True)
    scale = lax.rsqrt(total / (4 * width) + EPS)
    for piece, partner, offset in pieces:
        at = pl.multiple_of((head ^ partner) * width + offset, DH)
        cols = pl.ds(at, piece.shape[1])
        out_ref[:, cols] = (piece.astype(jnp.float32) * scale * gain_ref[:, cols]).astype(jnp.bfloat16)


def norm_rows(head, gain, share, row, own, mate, x2, x3, l2, l3, q2, q3, b2, b3, out):
    def at(pair, cols):
        index = pair[1] // HALF
        return pl.BlockSpec((HALF, cols), lambda n, s: (index, 0))

    def full(array):
        return pl.BlockSpec(array.shape, lambda n, s: (0, 0))

    width = own[0].shape[1]
    in_specs = [full(gain), at(own, width), at(mate, width), at(x2, width - DH), at(x3, width - DH)]
    in_specs += [at(l2, DH), at(l3, DH), at(q2, DH), at(q3, DH), full(b2), full(b3)]
    operands = [gain, own[0], mate[0], x2[0], x3[0], l2[0], l3[0], q2[0], q3[0], b2, b3]
    aliases = {}
    if out is not None:
        in_specs.append(pl.BlockSpec(memory_space=pl.ANY))
        operands.append(out)
        aliases = {len(operands): 0}
    index = row // HALF
    return pl.pallas_call(
        norm_kernel,
        grid_spec=pltpu.PrefetchScalarGridSpec(
            num_scalar_prefetch=1,
            grid=(1,),
            in_specs=in_specs,
            out_specs=pl.BlockSpec((HALF, 4 * width), lambda n, s: (index, 0)),
        ),
        out_shape=jax.ShapeDtypeStruct((share, 4 * width), jnp.bfloat16),
        input_output_aliases=aliases,
        compiler_params=params(),
        cost_estimate=COST,
        name="norm_rows",
    )(head, *operands)


def add_kernel(bit, with_before, mine_ref, total_ref, got_ref, *rest):
    group_ref, after_ref = rest[-2:]
    got = got_ref[...].astype(jnp.float32)
    late = jnp.where((mine_ref[0] & bit) > 0, got, 0.0)
    if with_before:
        late = late + rest[0][...]
    after_ref[...] = late
    group_ref[...] = (total_ref[...].astype(jnp.float32) + got).astype(jnp.bfloat16)


def add_step(mine, bit, total, got, before, tokens):
    vmem = pl.BlockSpec(memory_space=pltpu.VMEM)
    states = [total, got] + ([] if before is None else [before])
    return pl.pallas_call(
        functools.partial(add_kernel, bit, before is not None),
        in_specs=[pl.BlockSpec(memory_space=pltpu.SMEM)] + [vmem] * len(states)
        + [pl.BlockSpec(memory_space=pl.ANY)] * len(tokens),
        out_specs=[vmem, vmem],
        out_shape=[
            jax.ShapeDtypeStruct(total.shape, jnp.bfloat16),
            jax.ShapeDtypeStruct(total.shape, jnp.float32),
        ],
        compiler_params=params(),
        cost_estimate=COST,
        name="add_step",
    )(mine, *states, *tokens)


def swap(x, axis, size, bit):
    return lax.ppermute(x, axis, [(i, i ^ bit) for i in range(size)])


def across(pair):
    return [swap(x, "head", 4, k) for x, k in zip(pair, (2, 3))]


def shards(seq_size, queries, keys, values, norm_gain):
    rows, width = queries.shape
    heads = width // DH
    share = rows // 4
    units = share // HALF
    head = lax.axis_index("head")
    at = jnp.full((1,), head, jnp.int32)
    mine = jnp.full((1,), lax.axis_index("seq"), jnp.int32)
    gain = norm_gain.reshape(1, -1)
    far = (2, 3)

    slices = [lax.dynamic_slice(queries, ((head ^ k) * share, width - DH), (share, DH)) for k in far]
    early_q = across(slices)
    within, total, *early = block_states(at, keys, values, slices)
    early_l = [across([early[n], early[n + share // BLK]]) for n in range(share // BLK)]
    arrays = (queries, keys, values, within)
    group, before, bit, step = total, None, 1, 0
    while bit < seq_size:
        got = swap(group, "seq", seq_size, bit)
        tokens = []
        if step == 0:
            first = attention_rows(arrays, None, at, far, 0, BLK, 0, heads - 1, jnp.float32, [group])
            tokens = [*first, *early_q]
        elif step == 1:
            mate = attention_quarter(arrays, None, at, 1, jnp.float32, [group])
            tokens = [mate, *early_l[0]]
        elif step == 2:
            tokens = [*early_l[1]]
        group, before = add_step(mine, bit, group, got, before, tokens)
        bit, step = bit * 2, step + 1

    def far_unit(i, tokens, cost=None):
        return attention_rows(
            arrays, before, at, far, i * HALF, HALF, 0, heads - 1, jnp.bfloat16, tokens, cost
        )

    one = late_rows(queries, before, at, far, first, heads - 1, True, [])
    x1 = across(one)
    (mate,) = late_rows(queries, before, at, (1,), [mate], heads, False, one)
    mated = swap(mate, "head", 4, 1)
    two = far_unit(2, [mate])
    x2 = across(two)
    three = far_unit(3, [*two, *x1], LONG)
    x3 = across(three)
    own = attention_quarter(arrays, before, at, 0, jnp.bfloat16, three)
    x = [[(y, 0) for y in x1], [(y, HALF) for y in x1], [(y, 0) for y in x2], [(y, 0) for y in x3]]
    out = None
    for i in range(units):
        block, row = i * HALF // BLK, i * HALF % BLK
        out = norm_rows(
            at, gain, share, i * HALF, (own, i * HALF), (mated, i * HALF),
            x[i][0], x[i][1], (early_l[block][0], row), (early_l[block][1], row),
            (early_q[0], i * HALF), (early_q[1], i * HALF), x1[0], x1[1], out,
        )
    return out


def solution(mesh):
    seq_size = mesh.shape["seq"]

    def body(queries, keys, values, norm_gain):
        return shards(seq_size, queries, keys, values, norm_gain)

    return jax.shard_map(
        body,
        mesh=mesh,
        in_specs=(P("seq", "head"), P("seq", "head"), P("seq", "head"), P()),
        out_specs=P(("seq", "head"), None),
        check_vma=False,
    )
```

```python
import functools

import jax
import jax.numpy as jnp
from jax import lax
from jax.experimental import pallas as pl
from jax.experimental.pallas import tpu as pltpu
from jax.sharding import PartitionSpec as P

DH = 128
BLK = 512
HALF = 256
EXTRA = 48
TILE = 128
EPS = 1e-06
COST = pl.CostEstimate(flops=1024, bytes_accessed=1024, transcendentals=0)
LONG = pl.CostEstimate(flops=10**12, bytes_accessed=1024, transcendentals=0)


def params(mib=50):
    return pltpu.CompilerParams(vmem_limit_bytes=mib * 1024 * 1024)


def state_kernel(parts, tokens, k_ref, v_ref, *rest):
    within_ref, total_ref, k_buf, v_buf, k_sem, v_sem = rest[tokens:]
    rows, width = k_buf.shape
    heads, part = width // DH, rows // parts
    copies = []
    for p in range(parts):
        at = pl.ds(p * part, part)
        pair = (
            pltpu.make_async_copy(k_ref.at[at], k_buf.at[at], k_sem.at[p]),
            pltpu.make_async_copy(v_ref.at[at], v_buf.at[at], v_sem.at[p]),
        )
        for copy in pair:
            copy.start()
        copies.append(pair)
    acc = [jnp.zeros((DH, DH), jnp.float32) for _ in range(heads)]
    for p in range(parts):
        for copy in copies[p]:
            copy.wait()
        for n in range(p * part // BLK, (p + 1) * part // BLK):
            at = pl.ds(n * BLK, BLK)
            for h in range(heads):
                cols = pl.ds(h * DH, DH)
                within_ref[n, h] = acc[h]
                acc[h] = acc[h] + lax.dot_general(
                    k_buf[at, cols], v_buf[at, cols], (((0,), (0,)), ((), ())),
                    preferred_element_type=jnp.float32,
                )
    for h in range(heads):
        total_ref[h] = acc[h].astype(jnp.bfloat16)


def block_states(keys, values, *tokens):
    rows, width = keys.shape
    heads, blocks = width // DH, rows // BLK
    parts = 4 if blocks % 4 == 0 else 1
    anywhere = pl.BlockSpec(memory_space=pl.ANY)
    vmem = pl.BlockSpec(memory_space=pltpu.VMEM)
    return pl.pallas_call(
        functools.partial(state_kernel, parts, len(tokens)),
        in_specs=[anywhere, anywhere] + [anywhere] * len(tokens),
        out_specs=[vmem, vmem],
        out_shape=[
            jax.ShapeDtypeStruct((blocks, heads, DH, DH), jnp.float32),
            jax.ShapeDtypeStruct((heads, DH, DH), jnp.bfloat16),
        ],
        scratch_shapes=[
            pltpu.VMEM((rows, width), jnp.bfloat16),
            pltpu.VMEM((rows, width), jnp.bfloat16),
            pltpu.SemaphoreType.DMA((parts,)),
            pltpu.SemaphoreType.DMA((parts,)),
        ],
        compiler_params=params(),
        cost_estimate=COST,
        name="block_states",
    )(keys, values, *tokens)


def attend(first, halves, heads, q_ref, k_ref, v_ref, within_ref, before_ref, out_ref):
    row = lax.broadcasted_iota(jnp.int32, (HALF, HALF), 0)
    col = lax.broadcasted_iota(jnp.int32, (HALF, HALF), 1)
    for h in range(heads):
        cols = pl.ds(h * DH, DH)
        state = within_ref[0, h]
        if before_ref is not None:
            state = state + before_ref[h]
        q = q_ref[:, cols]
        out = jnp.dot(q, state.astype(jnp.bfloat16), preferred_element_type=jnp.float32)
        outs = [out[i * HALF:(i + 1) * HALF] for i in range(halves)]
        for j in range(first + halves):
            start = max(j - first, 0)
            there = pl.ds(j * HALF, HALF)
            scores = lax.dot_general(
                q[start * HALF:], k_ref[there, cols], (((1,), (1,)), ((), ())),
                preferred_element_type=jnp.float32,
            )
            low = []
            for i in range(start, halves):
                piece = scores[(i - start) * HALF:(i - start + 1) * HALF]
                if first + i == j:
                    piece = jnp.where(row >= col, piece, 0.0)
                low.append(piece.astype(jnp.bfloat16))
            low = jnp.concatenate(low, axis=0) if len(low) > 1 else low[0]
            more = jnp.dot(low, v_ref[there, cols], preferred_element_type=jnp.float32)
            for i in range(start, halves):
                outs[i] = outs[i] + more[(i - start) * HALF:(i - start + 1) * HALF]
        for i in range(halves):
            out_ref[pl.ds(i * HALF, HALF), cols] = outs[i].astype(out_ref.dtype)


def attention_rows(arrays, before, at, sides, start, size, head, heads, kind, tokens, cost=None):
    queries, keys, values, within = arrays
    rows, width = queries.shape
    share = rows // 4
    halves = size // HALF
    first = (start % BLK) // HALF
    k_rows = BLK if first + halves > 1 else HALF
    span = heads * DH
    across = head // heads
    count = len(sides)

    def quarter(n, s):
        side = sides[0]
        for i in range(1, count):
            side = jnp.where(n == i, sides[i], side)
        return s[0] ^ side

    def block(n, s):
        return quarter(n, s) * (share // BLK) + start // BLK

    keys_spec = pl.BlockSpec((k_rows, span), lambda n, s: (block(n, s) * (BLK // k_rows), across))
    in_specs = [
        pl.BlockSpec((size, span), lambda n, s: (quarter(n, s) * (share // size) + start // size, across)),
        keys_spec,
        keys_spec,
        pl.BlockSpec((1, heads, DH, DH), lambda n, s: (block(n, s), across, 0, 0)),
    ]
    operands = [queries, keys, values, within]
    if before is not None:
        in_specs.append(pl.BlockSpec(before.shape, lambda n, s: (0, 0, 0)))
        operands.append(before)
    in_specs += [pl.BlockSpec(memory_space=pl.ANY)] * len(tokens)

    def kernel(ids_ref, q_ref, k_ref, v_ref, within_ref, *rest):
        before_ref = None if before is None else rest[0]
        outs = rest[len(rest) - count:]
        for n in range(count):
            @pl.when(pl.program_id(0) == n)
            def _(n=n):
                attend(first, halves, heads, q_ref, k_ref, v_ref, within_ref, before_ref, outs[n])

    return pl.pallas_call(
        kernel,
        grid_spec=pltpu.PrefetchScalarGridSpec(
            num_scalar_prefetch=1,
            grid=(count,),
            in_specs=in_specs,
            out_specs=[pl.BlockSpec((size, span), lambda n, s: (0, 0))] * count,
        ),
        out_shape=[jax.ShapeDtypeStruct((size, span), kind)] * count,
        compiler_params=params(),
        cost_estimate=COST if cost is None else cost,
        name="attention_rows",
    )(at, *operands, *tokens)


def attention_quarter(arrays, before, at, side, kind, tokens):
    queries, keys, values, within = arrays
    rows, width = queries.shape
    share = rows // 4
    heads, blocks = width // DH, share // BLK
    block = pl.BlockSpec((BLK, width), lambda n, s: ((s[0] ^ side) * blocks + n, 0))
    state = pl.BlockSpec((1, heads, DH, DH), lambda n, s: ((s[0] ^ side) * blocks + n, 0, 0, 0))
    in_specs = [block, block, block, state]
    operands = [queries, keys, values, within]
    if before is not None:
        in_specs.append(pl.BlockSpec(before.shape, lambda n, s: (0, 0, 0)))
        operands.append(before)
    in_specs += [pl.BlockSpec(memory_space=pl.ANY)] * len(tokens)

    def kernel(quarter_ref, q_ref, k_ref, v_ref, within_ref, *rest):
        before_ref = None if before is None else rest[0]
        attend(0, BLK // HALF, heads, q_ref, k_ref, v_ref, within_ref, before_ref, rest[-1])

    return pl.pallas_call(
        kernel,
        grid_spec=pltpu.PrefetchScalarGridSpec(
            num_scalar_prefetch=1,
            grid=(blocks,),
            in_specs=in_specs,
            out_specs=pl.BlockSpec((BLK, width), lambda n, s: (n, 0)),
        ),
        out_shape=jax.ShapeDtypeStruct((share, width), kind),
        compiler_params=params(),
        cost_estimate=COST,
        name="attention_quarter",
    )(at, *operands, *tokens)


def early_kernel(tail, head_ref, q_ref, k_ref, v_ref, within_ref, *rest):
    outs = rest[len(rest) - 2:]
    if tail:
        tail_ref = rest[0]
    for side in range(2):
        @pl.when(pl.program_id(0) == side)
        def _(side=side):
            attend(0, BLK // HALF, 1, q_ref, k_ref, v_ref, within_ref, None, outs[side])
            if tail:
                outs[side][pl.ds(BLK, tail), :] = tail_ref[...]


def early_rows(head, queries, keys, values, within, n, tail, tokens):
    rows, width = keys.shape
    share, last = rows // 4, width // DH - 1
    blocks = share // BLK
    block = pl.BlockSpec((BLK, DH), lambda i, s: ((s[0] ^ (2 + i)) * blocks + n, last))
    in_specs = [
        block, block, block, pl.BlockSpec((1, 1, DH, DH), lambda i, s: ((s[0] ^ (2 + i)) * blocks + n, last, 0, 0)),
    ]
    operands = [queries, keys, values, within]
    if tail:
        per = share // tail
        in_specs.append(pl.BlockSpec((tail, DH), lambda i, s: ((s[0] ^ (2 + i)) * per + per - 1, last)))
        operands.append(queries)
    in_specs += [pl.BlockSpec(memory_space=pl.ANY)] * len(tokens)
    return pl.pallas_call(
        functools.partial(early_kernel, tail),
        grid_spec=pltpu.PrefetchScalarGridSpec(
            num_scalar_prefetch=1,
            grid=(2,),
            in_specs=in_specs,
            out_specs=[pl.BlockSpec((BLK + tail, DH), lambda i, s: (0, 0))] * 2,
        ),
        out_shape=[jax.ShapeDtypeStruct((BLK + tail, DH), jnp.bfloat16)] * 2,
        compiler_params=params(),
        cost_estimate=COST,
        name="early_rows",
    )(head, *operands, *tokens)


def late_kernel(count, heads, embed, bit, head_ref, *refs):
    before_ref = refs[2 * count]
    outs = refs[len(refs) - count:]
    if bit is not None:
        mine_ref, got_ref = refs[2 * count + 1:2 * count + 3]
        outs, after_ref = refs[len(refs) - count - 1:-1], refs[-1]
        after_ref[...] = before_ref[...] + jnp.where((mine_ref[0] & bit) > 0, got_ref[...].astype(jnp.float32), 0.0)
        before_ref = after_ref
    for n in range(count):
        q_ref, local_ref, out_ref = refs[2 * n], refs[2 * n + 1], outs[n]
        size = q_ref.shape[0]
        for h in range(heads):
            cols = pl.ds(h * DH, DH)
            out = local_ref[:, cols] + jnp.dot(
                q_ref[:, cols], before_ref[h].astype(jnp.bfloat16), preferred_element_type=jnp.float32
            )
            out_ref[pl.ds(0, size), cols] = out.astype(jnp.bfloat16)
        if embed:
            low = before_ref[heads].astype(jnp.bfloat16)
            for c in range(heads):
                high = min((c + 1) * EXTRA, DH)
                out_ref[pl.ds(size, high - c * EXTRA), pl.ds(c * DH, DH)] = low[c * EXTRA:high]


def late_rows(queries, before, at, sides, start, locals_, heads, embed, tokens, last=None):
    count = len(sides)
    size, span = locals_[0].shape
    steps = 1 if embed else size // BLK
    rows = size // steps
    share = queries.shape[0] // 4
    in_specs, operands = [], []
    for n in range(count):
        in_specs.append(pl.BlockSpec((rows, span), lambda i, s, side=sides[n]: ((s[0] ^ side) * (share // rows) + start // rows + i, 0)))
        in_specs.append(pl.BlockSpec((rows, span), lambda i, s: (i, 0)))
        operands += [queries, locals_[n]]
    state = pl.BlockSpec(before.shape, lambda i, s: (0, 0, 0))
    in_specs.append(state)
    operands.append(before)
    bit, out_specs, out_shape = None, [], []
    if last is not None:
        mine, bit, got = last
        in_specs += [pl.BlockSpec(memory_space=pltpu.SMEM), state]
        operands += [mine, got]
        out_specs, out_shape = [state], [jax.ShapeDtypeStruct(before.shape, jnp.float32)]
    in_specs += [pl.BlockSpec(memory_space=pl.ANY)] * len(tokens)
    more = EXTRA if embed else 0
    return pl.pallas_call(
        functools.partial(late_kernel, count, heads, embed, bit),
        grid_spec=pltpu.PrefetchScalarGridSpec(
            num_scalar_prefetch=1,
            grid=(steps,),
            in_specs=in_specs,
            out_specs=[pl.BlockSpec((rows + more, span), lambda i, s: (i, 0))] * count + out_specs,
        ),
        out_shape=[jax.ShapeDtypeStruct((size + more, span), jnp.bfloat16)] * count + out_shape,
        compiler_params=params(),
        cost_estimate=COST,
        name="late_rows",
    )(at, *operands, *tokens)


def early_out_kernel(l2_ref, l3_ref, q2_ref, q3_ref, b2_ref, b3_ref, o2_ref, o3_ref):
    for l_ref, q_ref, b_ref, o_ref in ((l2_ref, q2_ref, b2_ref, o2_ref), (l3_ref, q3_ref, b3_ref, o3_ref)):
        parts = []
        for c in range(b_ref.shape[1] // DH):
            high = min((c + 1) * EXTRA, DH)
            parts.append(b_ref[pl.ds(b_ref.shape[0] - EXTRA, high - c * EXTRA), pl.ds(c * DH, DH)])
        state = jnp.concatenate(parts, axis=0)
        out = l_ref[...].astype(jnp.float32) + jnp.dot(q_ref[...], state, preferred_element_type=jnp.float32)
        o_ref[...] = out.astype(jnp.bfloat16)


def early_out(size, l2, l3, q2, q3, b2, b3):
    def at(pair):
        index = pair[1] // size
        return pl.BlockSpec((size, DH), lambda n: (index, 0))

    def full(array):
        return pl.BlockSpec(array.shape, lambda n: (0, 0))

    out = jax.ShapeDtypeStruct((size, DH), jnp.bfloat16)
    return pl.pallas_call(
        early_out_kernel,
        grid=(1,),
        in_specs=[at(l2), at(l3), at(q2), at(q3), full(b2), full(b3)],
        out_specs=[pl.BlockSpec((size, DH), lambda n: (0, 0))] * 2,
        out_shape=[out, out],
        compiler_params=params(),
        cost_estimate=COST,
        name="early_out",
    )(l2[0], l3[0], q2[0], q3[0], b2, b3)


def norm_kernel(head_ref, gain_ref, own_ref, mate_ref, x2_ref, x3_ref, o2_ref, o3_ref, *rest):
    out_ref = rest[-1]
    head = head_ref[0]
    width = own_ref.shape[1]
    pieces = (
        (own_ref, 0, 0), (mate_ref, 1, 0), (x2_ref, 2, 0), (o2_ref, 2, width - DH), (x3_ref, 3, 0),
        (o3_ref, 3, width - DH),
    )
    total = 0.0
    for ref, _, _ in pieces:
        wide = ref[...].astype(jnp.float32)
        total += jnp.sum(wide * wide, axis=-1, keepdims=True)
    scale = lax.rsqrt(total / (4 * width) + EPS)
    for ref, partner, offset in pieces:
        at = pl.multiple_of((head ^ partner) * width + offset, DH)
        cols = pl.ds(at, ref.shape[1])
        out_ref[:, cols] = (ref[...].astype(jnp.float32) * scale * gain_ref[:, cols]).astype(jnp.bfloat16)


def norm_rows(head, gain, share, row, size, own, mate, x2, x3, o2, o3, out):
    def at(pair, cols):
        index = pair[1] // TILE
        return pl.BlockSpec((TILE, cols), lambda n, s: (index + n, 0))

    width = own[0].shape[1]
    in_specs = [pl.BlockSpec(gain.shape, lambda n, s: (0, 0)), at(own, width), at(mate, width)]
    in_specs += [at(x2, width - DH), at(x3, width - DH), at(o2, DH), at(o3, DH)]
    operands = [gain, own[0], mate[0], x2[0], x3[0], o2[0], o3[0]]
    aliases = {}
    if out is not None:
        in_specs.append(pl.BlockSpec(memory_space=pl.ANY))
        operands.append(out)
        aliases = {len(operands): 0}
    index = row // TILE
    return pl.pallas_call(
        norm_kernel,
        grid_spec=pltpu.PrefetchScalarGridSpec(
            num_scalar_prefetch=1,
            grid=(size // TILE,),
            in_specs=in_specs,
            out_specs=pl.BlockSpec((TILE, 4 * width), lambda n, s: (index + n, 0)),
        ),
        out_shape=jax.ShapeDtypeStruct((share, 4 * width), jnp.bfloat16),
        input_output_aliases=aliases,
        compiler_params=params(),
        cost_estimate=COST,
        name="norm_rows",
    )(head, *operands)


def add_kernel(bit, with_before, mine_ref, total_ref, got_ref, *rest):
    group_ref, after_ref = rest[-2:]
    got = got_ref[...].astype(jnp.float32)
    late = jnp.where((mine_ref[0] & bit) > 0, got, 0.0)
    if with_before:
        late = late + rest[0][...]
    after_ref[...] = late
    group_ref[...] = (total_ref[...].astype(jnp.float32) + got).astype(jnp.bfloat16)


def add_step(mine, bit, total, got, before, tokens):
    vmem = pl.BlockSpec(memory_space=pltpu.VMEM)
    states = [total, got] + ([] if before is None else [before])
    return pl.pallas_call(
        functools.partial(add_kernel, bit, before is not None),
        in_specs=[pl.BlockSpec(memory_space=pltpu.SMEM)] + [vmem] * len(states)
        + [pl.BlockSpec(memory_space=pl.ANY)] * len(tokens),
        out_specs=[vmem, vmem],
        out_shape=[
            jax.ShapeDtypeStruct(total.shape, jnp.bfloat16),
            jax.ShapeDtypeStruct(total.shape, jnp.float32),
        ],
        compiler_params=params(),
        cost_estimate=COST,
        name="add_step",
    )(mine, *states, *tokens)


def swap(x, axis, size, bit):
    return lax.ppermute(x, axis, [(i, i ^ bit) for i in range(size)])


def across(pair):
    return [swap(x, "head", 4, k) for x, k in zip(pair, (2, 3))]


def shards(seq_size, queries, keys, values, norm_gain):
    rows, width = queries.shape
    heads = width // DH
    share = rows // 4
    head = lax.axis_index("head")
    at = jnp.full((1,), head, jnp.int32)
    mine = jnp.full((1,), lax.axis_index("seq"), jnp.int32)
    gain = norm_gain.reshape(1, -1)
    far = (2, 3)

    tail = HALF
    slices = [lax.dynamic_slice(queries, ((head ^ k) * share, width - DH), (share - tail, DH)) for k in far]
    early_q = across(slices)
    within, total = block_states(keys, values, *slices)
    arrays = (queries, keys, values, within)
    group, before, bit, step = total, None, 1, 0
    early_l = []
    while bit < seq_size:
        got = swap(group, "seq", seq_size, bit)
        tokens = []
        if step < 2:
            early = early_rows(at, queries, keys, values, within, step, tail * step, [group])
            early_l.append(across(early))
            tokens = [*early, *(early_q if step == 0 else early_l[0])]
        elif step == 2:
            first = attention_rows(arrays, None, at, far, BLK, HALF, 0, heads - 1, jnp.float32, [group])
            tokens = [*first]
        if bit * 2 < seq_size:
            group, before = add_step(mine, bit, group, got, before, tokens)
        bit, step = bit * 2, step + 1

    def far_rows(start, size, tokens, cost=None):
        return attention_rows(arrays, before, at, far, start, size, 0, heads - 1, jnp.bfloat16, tokens, cost)

    *one, before = late_rows(queries, before, at, far, BLK, first, heads - 1, True, early_l[1], (mine, bit // 2, got))
    x1 = across(one)
    two = far_rows(0, BLK, one)
    x2 = across(two)
    mate = attention_quarter(arrays, before, at, 1, jnp.bfloat16, two)
    mated = swap(mate, "head", 4, 1)
    own = attention_quarter(arrays, before, at, 0, jnp.bfloat16, [mate])
    three = far_rows(BLK + HALF, HALF, [own, *x1], LONG)
    x3 = across(three)
    out = None
    low, high = early_l
    for row, size, (y2, y3) in ((BLK, HALF, x1), (0, BLK, x2), (BLK + HALF, HALF, x3)):
        l2, l3 = [(y, row) for y in low] if row < BLK else [(y, row - BLK) for y in high]
        q2, q3 = [(y, row) for y in early_q] if row < share - tail else [(y, BLK) for y in high]
        o2, o3 = early_out(size, l2, l3, q2, q3, x1[0], x1[1])
        out = norm_rows(
            at, gain, share, row, size, (own, row), (mated, row), (y2, 0), (y3, 0), (o2, 0), (o3, 0), out
        )
    return out


def solution(mesh):
    seq_size = mesh.shape["seq"]

    def body(queries, keys, values, norm_gain):
        return shards(seq_size, queries, keys, values, norm_gain)

    return jax.shard_map(
        body,
        mesh=mesh,
        in_specs=(P("seq", "head"), P("seq", "head"), P("seq", "head"), P()),
        out_specs=P(("seq", "head"), None),
        check_vma=False,
    )
```

```python
import functools

import jax
import jax.numpy as jnp
from jax import lax
from jax.experimental import pallas as pl
from jax.experimental.pallas import tpu as pltpu
from jax.sharding import PartitionSpec as P

DH = 128
BLK = 512
HALF = 256
EXTRA = 48
TILE = 128
EPS = 1e-06
COST = pl.CostEstimate(flops=1024, bytes_accessed=1024, transcendentals=0)
LONG = pl.CostEstimate(flops=10**12, bytes_accessed=1024, transcendentals=0)


def params(mib=50):
    return pltpu.CompilerParams(vmem_limit_bytes=mib * 1024 * 1024)


def state_kernel(parts, tokens, k_ref, v_ref, *rest):
    within_ref, total_ref, k_buf, v_buf, k_sem, v_sem = rest[tokens:]
    rows, width = k_buf.shape
    heads, part = width // DH, rows // parts
    copies = []
    for p in range(parts):
        at = pl.ds(p * part, part)
        pair = (
            pltpu.make_async_copy(k_ref.at[at], k_buf.at[at], k_sem.at[p]),
            pltpu.make_async_copy(v_ref.at[at], v_buf.at[at], v_sem.at[p]),
        )
        for copy in pair:
            copy.start()
        copies.append(pair)
    acc = [jnp.zeros((DH, DH), jnp.float32) for _ in range(heads)]
    for p in range(parts):
        for copy in copies[p]:
            copy.wait()
        for n in range(p * part // BLK, (p + 1) * part // BLK):
            at = pl.ds(n * BLK, BLK)
            for h in range(heads):
                cols = pl.ds(h * DH, DH)
                within_ref[n, h] = acc[h].astype(jnp.bfloat16)
                acc[h] = acc[h] + lax.dot_general(
                    k_buf[at, cols], v_buf[at, cols], (((0,), (0,)), ((), ())),
                    preferred_element_type=jnp.float32,
                )
    for h in range(heads):
        total_ref[h] = acc[h].astype(jnp.bfloat16)


def block_states(keys, values, *tokens):
    rows, width = keys.shape
    heads, blocks = width // DH, rows // BLK
    parts = 4 if blocks % 4 == 0 else 1
    anywhere = pl.BlockSpec(memory_space=pl.ANY)
    vmem = pl.BlockSpec(memory_space=pltpu.VMEM)
    return pl.pallas_call(
        functools.partial(state_kernel, parts, len(tokens)),
        in_specs=[anywhere, anywhere] + [anywhere] * len(tokens),
        out_specs=[vmem, vmem],
        out_shape=[
            jax.ShapeDtypeStruct((blocks, heads, DH, DH), jnp.bfloat16),
            jax.ShapeDtypeStruct((heads, DH, DH), jnp.bfloat16),
        ],
        scratch_shapes=[
            pltpu.VMEM((rows, width), jnp.bfloat16),
            pltpu.VMEM((rows, width), jnp.bfloat16),
            pltpu.SemaphoreType.DMA((parts,)),
            pltpu.SemaphoreType.DMA((parts,)),
        ],
        compiler_params=params(),
        cost_estimate=COST,
        name="block_states",
    )(keys, values, *tokens)


def attend(first, halves, heads, q_ref, k_ref, v_ref, within_ref, before_ref, *out_refs):
    row = lax.broadcasted_iota(jnp.int32, (HALF, HALF), 0)
    col = lax.broadcasted_iota(jnp.int32, (HALF, HALF), 1)
    for h in range(heads):
        cols = pl.ds(h * DH, DH)
        state = within_ref[0, h]
        if before_ref is not None:
            state = state.astype(jnp.float32) + before_ref[h]
        q = q_ref[:, cols]
        out = jnp.dot(q, state.astype(jnp.bfloat16), preferred_element_type=jnp.float32)
        outs = [out[i * HALF:(i + 1) * HALF] for i in range(halves)]
        for j in range(first + halves):
            start = max(j - first, 0)
            there = pl.ds(j * HALF, HALF)
            scores = lax.dot_general(
                q[start * HALF:], k_ref[there, cols], (((1,), (1,)), ((), ())),
                preferred_element_type=jnp.float32,
            )
            low = []
            for i in range(start, halves):
                piece = scores[(i - start) * HALF:(i - start + 1) * HALF]
                if first + i == j:
                    piece = jnp.where(row >= col, piece, 0.0)
                low.append(piece.astype(jnp.bfloat16))
            low = jnp.concatenate(low, axis=0) if len(low) > 1 else low[0]
            more = jnp.dot(low, v_ref[there, cols], preferred_element_type=jnp.float32)
            for i in range(start, halves):
                outs[i] = outs[i] + more[(i - start) * HALF:(i - start + 1) * HALF]
        for i in range(halves):
            part = HALF if len(out_refs) == 1 else HALF * halves // len(out_refs)
            for r in range(0, HALF, part):
                out_ref = out_refs[0] if len(out_refs) == 1 else out_refs[(i * HALF + r) // part]
                low_row = i * HALF if len(out_refs) == 1 else 0
                out_ref[pl.ds(low_row, part), cols] = outs[i][r:r + part].astype(out_ref.dtype)


def attention_rows(arrays, before, at, sides, start, size, head, heads, kind, tokens, cost=None, cut=1):
    queries, keys, values, within = arrays
    rows, width = queries.shape
    share = rows // 4
    halves = size // HALF
    first = (start % BLK) // HALF
    k_rows = BLK if first + halves > 1 else HALF
    span = heads * DH
    across = head // heads
    count = len(sides)

    def quarter(n, s):
        side = sides[0]
        for i in range(1, count):
            side = jnp.where(n == i, sides[i], side)
        return s[0] ^ side

    def block(n, s):
        return quarter(n, s) * (share // BLK) + start // BLK

    keys_spec = pl.BlockSpec((k_rows, span), lambda n, s: (block(n, s) * (BLK // k_rows), across))
    in_specs = [
        pl.BlockSpec((size, span), lambda n, s: (quarter(n, s) * (share // size) + start // size, across)),
        keys_spec,
        keys_spec,
        pl.BlockSpec((1, heads, DH, DH), lambda n, s: (block(n, s), across, 0, 0)),
    ]
    operands = [queries, keys, values, within]
    if before is not None:
        in_specs.append(pl.BlockSpec(before.shape, lambda n, s: (0, 0, 0)))
        operands.append(before)
    in_specs += [pl.BlockSpec(memory_space=pl.ANY)] * len(tokens)

    def kernel(ids_ref, q_ref, k_ref, v_ref, within_ref, *rest):
        before_ref = None if before is None else rest[0]
        outs = rest[len(rest) - count * cut:]
        for n in range(count):
            @pl.when(pl.program_id(0) == n)
            def _(n=n):
                mine = outs[n * cut:(n + 1) * cut]
                attend(first, halves, heads, q_ref, k_ref, v_ref, within_ref, before_ref, *mine)

    return pl.pallas_call(
        kernel,
        grid_spec=pltpu.PrefetchScalarGridSpec(
            num_scalar_prefetch=1,
            grid=(count,),
            in_specs=in_specs,
            out_specs=[pl.BlockSpec((size // cut, span), lambda n, s: (0, 0))] * (count * cut),
        ),
        out_shape=[jax.ShapeDtypeStruct((size // cut, span), kind)] * (count * cut),
        compiler_params=params(),
        cost_estimate=COST if cost is None else cost,
        name="attention_rows",
    )(at, *operands, *tokens)


def attention_quarter(arrays, before, at, side, kind, tokens):
    queries, keys, values, within = arrays
    rows, width = queries.shape
    share = rows // 4
    heads, blocks = width // DH, share // BLK
    block = pl.BlockSpec((BLK, width), lambda n, s: ((s[0] ^ side) * blocks + n, 0))
    state = pl.BlockSpec((1, heads, DH, DH), lambda n, s: ((s[0] ^ side) * blocks + n, 0, 0, 0))
    in_specs = [block, block, block, state]
    operands = [queries, keys, values, within]
    if before is not None:
        in_specs.append(pl.BlockSpec(before.shape, lambda n, s: (0, 0, 0)))
        operands.append(before)
    in_specs += [pl.BlockSpec(memory_space=pl.ANY)] * len(tokens)

    def kernel(quarter_ref, q_ref, k_ref, v_ref, within_ref, *rest):
        before_ref = None if before is None else rest[0]
        attend(0, BLK // HALF, heads, q_ref, k_ref, v_ref, within_ref, before_ref, rest[-1])

    return pl.pallas_call(
        kernel,
        grid_spec=pltpu.PrefetchScalarGridSpec(
            num_scalar_prefetch=1,
            grid=(blocks,),
            in_specs=in_specs,
            out_specs=pl.BlockSpec((BLK, width), lambda n, s: (n, 0)),
        ),
        out_shape=jax.ShapeDtypeStruct((share, width), kind),
        compiler_params=params(),
        cost_estimate=COST,
        name="attention_quarter",
    )(at, *operands, *tokens)


def early_kernel(tail, head_ref, q_ref, k_ref, v_ref, within_ref, *rest):
    outs = rest[len(rest) - 2:]
    if tail:
        tail_ref = rest[0]
    for side in range(2):
        @pl.when(pl.program_id(0) == side)
        def _(side=side):
            attend(0, BLK // HALF, 1, q_ref, k_ref, v_ref, within_ref, None, outs[side])
            if tail:
                outs[side][pl.ds(BLK, tail), :] = tail_ref[...]


def early_rows(head, queries, keys, values, within, n, tail, tokens):
    rows, width = keys.shape
    share, last = rows // 4, width // DH - 1
    blocks = share // BLK
    block = pl.BlockSpec((BLK, DH), lambda i, s: ((s[0] ^ (2 + i)) * blocks + n, last))
    in_specs = [
        block, block, block, pl.BlockSpec((1, 1, DH, DH), lambda i, s: ((s[0] ^ (2 + i)) * blocks + n, last, 0, 0)),
    ]
    operands = [queries, keys, values, within]
    if tail:
        per = share // tail
        in_specs.append(pl.BlockSpec((tail, DH), lambda i, s: ((s[0] ^ (2 + i)) * per + per - 1, last)))
        operands.append(queries)
    in_specs += [pl.BlockSpec(memory_space=pl.ANY)] * len(tokens)
    return pl.pallas_call(
        functools.partial(early_kernel, tail),
        grid_spec=pltpu.PrefetchScalarGridSpec(
            num_scalar_prefetch=1,
            grid=(2,),
            in_specs=in_specs,
            out_specs=[pl.BlockSpec((BLK + tail, DH), lambda i, s: (0, 0))] * 2,
        ),
        out_shape=[jax.ShapeDtypeStruct((BLK + tail, DH), jnp.bfloat16)] * 2,
        compiler_params=params(),
        cost_estimate=COST,
        name="early_rows",
    )(head, *operands, *tokens)


def late_kernel(count, heads, embed, bit, head_ref, *refs):
    before_ref = refs[2 * count]
    outs = refs[len(refs) - count:]
    if bit is not None:
        mine_ref, got_ref = refs[2 * count + 1:2 * count + 3]
        outs, after_ref = refs[len(refs) - count - 1:-1], refs[-1]
        after_ref[...] = before_ref[...] + jnp.where((mine_ref[0] & bit) > 0, got_ref[...].astype(jnp.float32), 0.0)
        before_ref = after_ref
    for n in range(count):
        q_ref, local_ref, out_ref = refs[2 * n], refs[2 * n + 1], outs[n]
        size = q_ref.shape[0]
        for h in range(heads):
            cols = pl.ds(h * DH, DH)
            out = local_ref[:, cols] + jnp.dot(
                q_ref[:, cols], before_ref[h].astype(jnp.bfloat16), preferred_element_type=jnp.float32
            )
            out_ref[pl.ds(0, size), cols] = out.astype(jnp.bfloat16)
        if embed:
            low = before_ref[heads].astype(jnp.bfloat16)
            for c in range(heads):
                high = min((c + 1) * EXTRA, DH)
                out_ref[pl.ds(size, high - c * EXTRA), pl.ds(c * DH, DH)] = low[c * EXTRA:high]


def late_rows(queries, before, at, sides, start, locals_, heads, embed, tokens, last=None):
    count = len(sides)
    size, span = locals_[0].shape
    steps = 1 if embed else size // BLK
    rows = size // steps
    share = queries.shape[0] // 4
    in_specs, operands = [], []
    for n in range(count):
        in_specs.append(pl.BlockSpec((rows, span), lambda i, s, side=sides[n]: ((s[0] ^ side) * (share // rows) + start // rows + i, 0)))
        in_specs.append(pl.BlockSpec((rows, span), lambda i, s: (i, 0)))
        operands += [queries, locals_[n]]
    state = pl.BlockSpec(before.shape, lambda i, s: (0, 0, 0))
    in_specs.append(state)
    operands.append(before)
    bit, out_specs, out_shape = None, [], []
    if last is not None:
        mine, bit, got = last
        in_specs += [pl.BlockSpec(memory_space=pltpu.SMEM), state]
        operands += [mine, got]
        out_specs, out_shape = [state], [jax.ShapeDtypeStruct(before.shape, jnp.float32)]
    in_specs += [pl.BlockSpec(memory_space=pl.ANY)] * len(tokens)
    more = EXTRA if embed else 0
    return pl.pallas_call(
        functools.partial(late_kernel, count, heads, embed, bit),
        grid_spec=pltpu.PrefetchScalarGridSpec(
            num_scalar_prefetch=1,
            grid=(steps,),
            in_specs=in_specs,
            out_specs=[pl.BlockSpec((rows + more, span), lambda i, s: (i, 0))] * count + out_specs,
        ),
        out_shape=[jax.ShapeDtypeStruct((size + more, span), jnp.bfloat16)] * count + out_shape,
        compiler_params=params(),
        cost_estimate=COST,
        name="late_rows",
    )(at, *operands, *tokens)


def early_out_kernel(l2_ref, l3_ref, q2_ref, q3_ref, b2_ref, b3_ref, o2_ref, o3_ref):
    for l_ref, q_ref, b_ref, o_ref in ((l2_ref, q2_ref, b2_ref, o2_ref), (l3_ref, q3_ref, b3_ref, o3_ref)):
        parts = []
        for c in range(b_ref.shape[1] // DH):
            high = min((c + 1) * EXTRA, DH)
            parts.append(b_ref[pl.ds(b_ref.shape[0] - EXTRA, high - c * EXTRA), pl.ds(c * DH, DH)])
        state = jnp.concatenate(parts, axis=0)
        out = l_ref[...].astype(jnp.float32) + jnp.dot(q_ref[...], state, preferred_element_type=jnp.float32)
        o_ref[...] = out.astype(jnp.bfloat16)


def early_out(size, l2, l3, q2, q3, b2, b3):
    def at(pair):
        index = pair[1] // size
        return pl.BlockSpec((size, DH), lambda n: (index, 0))

    def full(array):
        return pl.BlockSpec(array.shape, lambda n: (0, 0))

    out = jax.ShapeDtypeStruct((size, DH), jnp.bfloat16)
    return pl.pallas_call(
        early_out_kernel,
        grid=(1,),
        in_specs=[at(l2), at(l3), at(q2), at(q3), full(b2), full(b3)],
        out_specs=[pl.BlockSpec((size, DH), lambda n: (0, 0))] * 2,
        out_shape=[out, out],
        compiler_params=params(),
        cost_estimate=COST,
        name="early_out",
    )(l2[0], l3[0], q2[0], q3[0], b2, b3)


def gather_kernel(own_ref, mate_ref, o2_ref, o3_ref, out_ref):
    first = 0
    for ref in (own_ref, mate_ref, o2_ref, o3_ref):
        out_ref[:, pl.ds(first, ref.shape[1])] = ref[...]
        first += ref.shape[1]


def gather_rows(size, *pairs):
    def at(pair):
        index = pair[1] // size
        return pl.BlockSpec((size, pair[0].shape[1]), lambda n: (index, 0))

    width = sum(pair[0].shape[1] for pair in pairs)
    return pl.pallas_call(
        gather_kernel,
        grid=(1,),
        in_specs=[at(pair) for pair in pairs],
        out_specs=pl.BlockSpec((size, width), lambda n: (0, 0)),
        out_shape=jax.ShapeDtypeStruct((size, width), jnp.bfloat16),
        compiler_params=params(),
        cost_estimate=COST,
        name="gather_rows",
    )(*[pair[0] for pair in pairs])


def norm_last(head, gain, share, row, near, x2, x3, out):
    size, narrow = x2.shape
    width = narrow + DH
    index = row // size
    vmem = pl.BlockSpec(memory_space=pltpu.VMEM)

    def kernel(head_ref, gain_ref, near_ref, x2_ref, x3_ref, old_ref, out_ref):
        cut = [0, width, 2 * width, 2 * width + DH, 2 * width + 2 * DH]
        refs = [near_ref.at[:, pl.ds(a, b - a)] for a, b in zip(cut, cut[1:])]
        norm_kernel(head_ref, gain_ref, refs[0], refs[1], x2_ref, x3_ref, refs[2], refs[3], out_ref)

    return pl.pallas_call(
        kernel,
        grid_spec=pltpu.PrefetchScalarGridSpec(
            num_scalar_prefetch=1,
            grid=(1,),
            in_specs=[vmem] * 4 + [pl.BlockSpec(memory_space=pl.ANY)],
            out_specs=pl.BlockSpec((size, 4 * width), lambda n, s: (index, 0)),
        ),
        out_shape=jax.ShapeDtypeStruct((share, 4 * width), jnp.bfloat16),
        input_output_aliases={5: 0},
        compiler_params=params(),
        cost_estimate=COST,
        name="norm_last",
    )(head, gain, near, x2, x3, out)


def norm_kernel(head_ref, gain_ref, own_ref, mate_ref, x2_ref, x3_ref, o2_ref, o3_ref, *rest):
    out_ref = rest[-1]
    head = head_ref[0]
    width = own_ref.shape[1]
    pieces = (
        (own_ref, 0, 0), (mate_ref, 1, 0), (x2_ref, 2, 0), (o2_ref, 2, width - DH), (x3_ref, 3, 0),
        (o3_ref, 3, width - DH),
    )
    total = jnp.zeros((own_ref.shape[0], DH), jnp.float32)
    for ref, _, _ in pieces:
        for c in range(ref.shape[1] // DH):
            wide = ref[:, pl.ds(c * DH, DH)].astype(jnp.float32)
            total += wide * wide
    total = jnp.sum(total, axis=-1, keepdims=True)
    scale = lax.rsqrt(total / (4 * width) + EPS)
    for ref, partner, offset in pieces:
        at = pl.multiple_of((head ^ partner) * width + offset, DH)
        cols = pl.ds(at, ref.shape[1])
        out_ref[:, cols] = (ref[...].astype(jnp.float32) * scale * gain_ref[:, cols]).astype(jnp.bfloat16)


def norm_rows(head, gain, share, row, size, own, mate, x2, x3, o2, o3, out):
    def at(pair, cols):
        index = pair[1] // TILE
        return pl.BlockSpec((TILE, cols), lambda n, s: (index + n, 0))

    width = own[0].shape[1]
    in_specs = [pl.BlockSpec(gain.shape, lambda n, s: (0, 0)), at(own, width), at(mate, width)]
    in_specs += [at(x2, width - DH), at(x3, width - DH), at(o2, DH), at(o3, DH)]
    operands = [gain, own[0], mate[0], x2[0], x3[0], o2[0], o3[0]]
    aliases = {}
    if out is not None:
        in_specs.append(pl.BlockSpec(memory_space=pl.ANY))
        operands.append(out)
        aliases = {len(operands): 0}
    index = row // TILE
    return pl.pallas_call(
        norm_kernel,
        grid_spec=pltpu.PrefetchScalarGridSpec(
            num_scalar_prefetch=1,
            grid=(size // TILE,),
            in_specs=in_specs,
            out_specs=pl.BlockSpec((TILE, 4 * width), lambda n, s: (index + n, 0)),
        ),
        out_shape=jax.ShapeDtypeStruct((share, 4 * width), jnp.bfloat16),
        input_output_aliases=aliases,
        compiler_params=params(),
        cost_estimate=COST,
        name="norm_rows",
    )(head, *operands)


def add_kernel(bit, with_before, mine_ref, total_ref, got_ref, *rest):
    group_ref, after_ref = rest[-2:]
    got = got_ref[...].astype(jnp.float32)
    late = jnp.where((mine_ref[0] & bit) > 0, got, 0.0)
    if with_before:
        late = late + rest[0][...]
    after_ref[...] = late
    group_ref[...] = (total_ref[...].astype(jnp.float32) + got).astype(jnp.bfloat16)


def add_step(mine, bit, total, got, before, tokens):
    vmem = pl.BlockSpec(memory_space=pltpu.VMEM)
    states = [total, got] + ([] if before is None else [before])
    return pl.pallas_call(
        functools.partial(add_kernel, bit, before is not None),
        in_specs=[pl.BlockSpec(memory_space=pltpu.SMEM)] + [vmem] * len(states)
        + [pl.BlockSpec(memory_space=pl.ANY)] * len(tokens),
        out_specs=[vmem, vmem],
        out_shape=[
            jax.ShapeDtypeStruct(total.shape, jnp.bfloat16),
            jax.ShapeDtypeStruct(total.shape, jnp.float32),
        ],
        compiler_params=params(),
        cost_estimate=COST,
        name="add_step",
    )(mine, *states, *tokens)


def swap(x, axis, size, bit):
    return lax.ppermute(x, axis, [(i, i ^ bit) for i in range(size)])


def across(pair):
    return [swap(x, "head", 4, k) for x, k in zip(pair, (2, 3))]


def shards(seq_size, queries, keys, values, norm_gain):
    rows, width = queries.shape
    heads = width // DH
    share = rows // 4
    head = lax.axis_index("head")
    at = jnp.full((1,), head, jnp.int32)
    mine = jnp.full((1,), lax.axis_index("seq"), jnp.int32)
    gain = norm_gain.reshape(1, -1)
    far = (2, 3)

    tail = HALF
    slices = [lax.dynamic_slice(queries, ((head ^ k) * share, width - DH), (share - tail, DH)) for k in far]
    early_q = across(slices)
    within, total = block_states(keys, values, *slices)
    arrays = (queries, keys, values, within)
    group, before, bit, step = total, None, 1, 0
    early_l = []
    while bit < seq_size:
        got = swap(group, "seq", seq_size, bit)
        tokens = []
        if step < 2:
            early = early_rows(at, queries, keys, values, within, step, tail * step, [group])
            early_l.append(across(early))
            tokens = [*early, *(early_q if step == 0 else early_l[0])]
        elif step == 2:
            first = attention_rows(arrays, None, at, far, BLK, HALF, 0, heads - 1, jnp.float32, [group])
            tokens = [*first]
        if bit * 2 < seq_size:
            group, before = add_step(mine, bit, group, got, before, tokens)
        bit, step = bit * 2, step + 1

    def far_rows(start, size, tokens, cost=None, cut=1):
        return attention_rows(arrays, before, at, far, start, size, 0, heads - 1, jnp.bfloat16, tokens, cost, cut)

    *one, before = late_rows(queries, before, at, far, BLK, first, heads - 1, True, early_l[1], (mine, bit // 2, got))
    x1 = across(one)
    two = far_rows(0, BLK, one)
    x2 = across(two)
    mate = attention_quarter(arrays, before, at, 1, jnp.bfloat16, two)
    mated = swap(mate, "head", 4, 1)
    own = attention_quarter(arrays, before, at, 0, jnp.bfloat16, [mate])
    three = far_rows(BLK + HALF, HALF, [own, *x1], LONG, 2)
    x3, x4 = across(three[0::2]), across(three[1::2])
    out = None
    low, high = early_l
    end = share - HALF // 2
    for row, size, (y2, y3) in ((BLK, HALF, x1), (0, BLK, x2), (BLK + HALF, HALF, x3)):
        l2, l3 = [(y, row) for y in low] if row < BLK else [(y, row - BLK) for y in high]
        q2, q3 = [(y, row) for y in early_q] if row < share - tail else [(y, BLK) for y in high]
        o2, o3 = early_out(size, l2, l3, q2, q3, x1[0], x1[1])
        size = min(size, end - row)
        out = norm_rows(
            at, gain, share, row, size, (own, row), (mated, row), (y2, 0), (y3, 0), (o2, 0), (o3, 0), out
        )
    near = gather_rows(share - end, (own, end), (mated, end), (o2, HALF // 2), (o3, HALF // 2))
    return norm_last(at, gain, share, end, near, x4[0], x4[1], out)


def solution(mesh):
    seq_size = mesh.shape["seq"]

    def body(queries, keys, values, norm_gain):
        return shards(seq_size, queries, keys, values, norm_gain)

    return jax.shard_map(
        body,
        mesh=mesh,
        in_specs=(P("seq", "head"), P("seq", "head"), P("seq", "head"), P()),
        out_specs=P(("seq", "head"), None),
        check_vma=False,
    )
```

```python
import functools

import jax
import jax.numpy as jnp
from jax import lax
from jax.experimental import pallas as pl
from jax.experimental.pallas import tpu as pltpu
from jax.sharding import PartitionSpec as P

DH = 128
BLK = 512
HALF = 256
EXTRA = 48
TILE = 128
EPS = 1e-06
COST = pl.CostEstimate(flops=1024, bytes_accessed=1024, transcendentals=0)
LONG = pl.CostEstimate(flops=10**12, bytes_accessed=1024, transcendentals=0)


def params(mib=50):
    return pltpu.CompilerParams(vmem_limit_bytes=mib * 1024 * 1024)


def state_kernel(parts, tokens, k_ref, v_ref, *rest):
    within_ref, total_ref, k_buf, v_buf, k_sem, v_sem = rest[tokens:]
    rows, width = k_buf.shape
    heads, part = width // DH, rows // parts
    copies = []
    for p in range(parts):
        at = pl.ds(p * part, part)
        pair = (
            pltpu.make_async_copy(k_ref.at[at], k_buf.at[at], k_sem.at[p]),
            pltpu.make_async_copy(v_ref.at[at], v_buf.at[at], v_sem.at[p]),
        )
        for copy in pair:
            copy.start()
        copies.append(pair)
    acc = [jnp.zeros((DH, DH), jnp.float32) for _ in range(heads)]
    for p in range(parts):
        for copy in copies[p]:
            copy.wait()
        for n in range(p * part // BLK, (p + 1) * part // BLK):
            at = pl.ds(n * BLK, BLK)
            for h in range(heads):
                cols = pl.ds(h * DH, DH)
                within_ref[n, h] = acc[h].astype(jnp.bfloat16)
                acc[h] = acc[h] + lax.dot_general(
                    k_buf[at, cols], v_buf[at, cols], (((0,), (0,)), ((), ())),
                    preferred_element_type=jnp.float32,
                )
    for h in range(heads):
        total_ref[h] = acc[h].astype(jnp.bfloat16)


def block_states(keys, values, *tokens):
    rows, width = keys.shape
    heads, blocks = width // DH, rows // BLK
    parts = 4 if blocks % 4 == 0 else 1
    anywhere = pl.BlockSpec(memory_space=pl.ANY)
    vmem = pl.BlockSpec(memory_space=pltpu.VMEM)
    return pl.pallas_call(
        functools.partial(state_kernel, parts, len(tokens)),
        in_specs=[anywhere, anywhere] + [anywhere] * len(tokens),
        out_specs=[vmem, vmem],
        out_shape=[
            jax.ShapeDtypeStruct((blocks, heads, DH, DH), jnp.bfloat16),
            jax.ShapeDtypeStruct((heads, DH, DH), jnp.bfloat16),
        ],
        scratch_shapes=[
            pltpu.VMEM((rows, width), jnp.bfloat16),
            pltpu.VMEM((rows, width), jnp.bfloat16),
            pltpu.SemaphoreType.DMA((parts,)),
            pltpu.SemaphoreType.DMA((parts,)),
        ],
        compiler_params=params(),
        cost_estimate=COST,
        name="block_states",
    )(keys, values, *tokens)


def attend(first, halves, heads, q_ref, k_ref, v_ref, within_ref, before_ref, *out_refs):
    row = lax.broadcasted_iota(jnp.int32, (HALF, HALF), 0)
    col = lax.broadcasted_iota(jnp.int32, (HALF, HALF), 1)
    for h in range(heads):
        cols = pl.ds(h * DH, DH)
        state = within_ref[0, h]
        if before_ref is not None:
            state = state.astype(jnp.float32) + before_ref[h]
        q = q_ref[:, cols]
        out = jnp.dot(q, state.astype(jnp.bfloat16), preferred_element_type=jnp.float32)
        outs = [out[i * HALF:(i + 1) * HALF] for i in range(halves)]
        for j in range(first + halves):
            start = max(j - first, 0)
            there = pl.ds(j * HALF, HALF)
            scores = lax.dot_general(
                q[start * HALF:], k_ref[there, cols], (((1,), (1,)), ((), ())),
                preferred_element_type=jnp.float32,
            )
            low = []
            for i in range(start, halves):
                piece = scores[(i - start) * HALF:(i - start + 1) * HALF]
                if first + i == j:
                    piece = jnp.where(row >= col, piece, 0.0)
                low.append(piece.astype(jnp.bfloat16))
            low = jnp.concatenate(low, axis=0) if len(low) > 1 else low[0]
            more = jnp.dot(low, v_ref[there, cols], preferred_element_type=jnp.float32)
            for i in range(start, halves):
                outs[i] = outs[i] + more[(i - start) * HALF:(i - start + 1) * HALF]
        for i in range(halves):
            part = HALF if len(out_refs) == 1 else HALF * halves // len(out_refs)
            for r in range(0, HALF, part):
                out_ref = out_refs[0] if len(out_refs) == 1 else out_refs[(i * HALF + r) // part]
                low_row = i * HALF if len(out_refs) == 1 else 0
                out_ref[pl.ds(low_row, part), cols] = outs[i][r:r + part].astype(out_ref.dtype)


def attention_rows(arrays, before, at, sides, start, size, head, heads, kind, tokens, cost=None, cut=1, keep=False):
    queries, keys, values, within = arrays
    rows, width = queries.shape
    share = rows // 4
    halves = size // HALF
    first = (start % BLK) // HALF
    k_rows = BLK if first + halves > 1 else HALF
    span = heads * DH
    across = head // heads
    count = len(sides)

    def quarter(n, s):
        side = sides[0]
        for i in range(1, count):
            side = jnp.where(n == i, sides[i], side)
        return s[0] ^ side

    def block(n, s):
        return quarter(n, s) * (share // BLK) + start // BLK

    keys_spec = pl.BlockSpec((k_rows, span), lambda n, s: (block(n, s) * (BLK // k_rows), across))
    in_specs = [
        pl.BlockSpec((size, span), lambda n, s: (quarter(n, s) * (share // size) + start // size, across)),
        keys_spec,
        keys_spec,
        pl.BlockSpec((1, heads, DH, DH), lambda n, s: (block(n, s), across, 0, 0)),
    ]
    operands = [queries, keys, values, within]
    if before is not None:
        in_specs.append(pl.BlockSpec(before.shape, lambda n, s: (0, 0, 0)))
        operands.append(before)
    in_specs += [pl.BlockSpec(memory_space=pl.ANY)] * len(tokens)

    def kernel(ids_ref, q_ref, k_ref, v_ref, within_ref, *rest):
        before_ref = None if before is None else rest[0]
        outs = rest[len(rest) - count * (cut + keep):]
        for n in range(count):
            @pl.when(pl.program_id(0) == n)
            def _(n=n):
                mine = outs[n * cut:(n + 1) * cut]
                attend(first, halves, heads, q_ref, k_ref, v_ref, within_ref, before_ref, *mine)
                if keep:
                    outs[count * cut + n][...] = q_ref[...]

    return pl.pallas_call(
        kernel,
        grid_spec=pltpu.PrefetchScalarGridSpec(
            num_scalar_prefetch=1,
            grid=(count,),
            in_specs=in_specs,
            out_specs=[pl.BlockSpec((size // cut, span), lambda n, s: (0, 0))] * (count * (cut + keep)),
        ),
        out_shape=[jax.ShapeDtypeStruct((size // cut, span), kind)] * (count * cut)
        + [jax.ShapeDtypeStruct((size, span), jnp.bfloat16)] * (count * keep),
        compiler_params=params(),
        cost_estimate=COST if cost is None else cost,
        name="attention_rows",
    )(at, *operands, *tokens)


def attention_quarter(arrays, before, at, side, kind, tokens):
    queries, keys, values, within = arrays
    rows, width = queries.shape
    share = rows // 4
    heads, blocks = width // DH, share // BLK
    block = pl.BlockSpec((BLK, width), lambda n, s: ((s[0] ^ side) * blocks + n, 0))
    state = pl.BlockSpec((1, heads, DH, DH), lambda n, s: ((s[0] ^ side) * blocks + n, 0, 0, 0))
    in_specs = [block, block, block, state]
    operands = [queries, keys, values, within]
    if before is not None:
        in_specs.append(pl.BlockSpec(before.shape, lambda n, s: (0, 0, 0)))
        operands.append(before)
    in_specs += [pl.BlockSpec(memory_space=pl.ANY)] * len(tokens)

    def kernel(quarter_ref, q_ref, k_ref, v_ref, within_ref, *rest):
        before_ref = None if before is None else rest[0]
        attend(0, BLK // HALF, heads, q_ref, k_ref, v_ref, within_ref, before_ref, rest[-1])

    return pl.pallas_call(
        kernel,
        grid_spec=pltpu.PrefetchScalarGridSpec(
            num_scalar_prefetch=1,
            grid=(blocks,),
            in_specs=in_specs,
            out_specs=pl.BlockSpec((BLK, width), lambda n, s: (n, 0)),
        ),
        out_shape=jax.ShapeDtypeStruct((share, width), kind),
        compiler_params=params(),
        cost_estimate=COST,
        name="attention_quarter",
    )(at, *operands, *tokens)


def early_kernel(tail, head_ref, q_ref, k_ref, v_ref, within_ref, *rest):
    outs = rest[len(rest) - 2:]
    if tail:
        tail_ref = rest[0]
    for side in range(2):
        @pl.when(pl.program_id(0) == side)
        def _(side=side):
            attend(0, BLK // HALF, 1, q_ref, k_ref, v_ref, within_ref, None, outs[side])
            if tail:
                outs[side][pl.ds(BLK, tail), :] = tail_ref[...]


def early_rows(head, queries, keys, values, within, n, tail, tokens):
    rows, width = keys.shape
    share, last = rows // 4, width // DH - 1
    blocks = share // BLK
    block = pl.BlockSpec((BLK, DH), lambda i, s: ((s[0] ^ (2 + i)) * blocks + n, last))
    in_specs = [
        block, block, block, pl.BlockSpec((1, 1, DH, DH), lambda i, s: ((s[0] ^ (2 + i)) * blocks + n, last, 0, 0)),
    ]
    operands = [queries, keys, values, within]
    if tail:
        per = share // tail
        in_specs.append(pl.BlockSpec((tail, DH), lambda i, s: ((s[0] ^ (2 + i)) * per + per - 1, last)))
        operands.append(queries)
    in_specs += [pl.BlockSpec(memory_space=pl.ANY)] * len(tokens)
    return pl.pallas_call(
        functools.partial(early_kernel, tail),
        grid_spec=pltpu.PrefetchScalarGridSpec(
            num_scalar_prefetch=1,
            grid=(2,),
            in_specs=in_specs,
            out_specs=[pl.BlockSpec((BLK + tail, DH), lambda i, s: (0, 0))] * 2,
        ),
        out_shape=[jax.ShapeDtypeStruct((BLK + tail, DH), jnp.bfloat16)] * 2,
        compiler_params=params(),
        cost_estimate=COST,
        name="early_rows",
    )(head, *operands, *tokens)


def late_kernel(count, heads, embed, bit, head_ref, *refs):
    before_ref = refs[2 * count]
    outs = refs[len(refs) - count:]
    if bit is not None:
        mine_ref, got_ref = refs[2 * count + 1:2 * count + 3]
        outs, after_ref = refs[len(refs) - count - 1:-1], refs[-1]
        after_ref[...] = before_ref[...] + jnp.where((mine_ref[0] & bit) > 0, got_ref[...].astype(jnp.float32), 0.0)
        before_ref = after_ref
    for n in range(count):
        q_ref, local_ref, out_ref = refs[2 * n], refs[2 * n + 1], outs[n]
        size = q_ref.shape[0]
        for h in range(heads):
            cols = pl.ds(h * DH, DH)
            out = local_ref[:, cols].astype(jnp.float32) + jnp.dot(
                q_ref[:, cols], before_ref[h].astype(jnp.bfloat16), preferred_element_type=jnp.float32
            )
            out_ref[pl.ds(0, size), cols] = out.astype(jnp.bfloat16)
        if embed and n == 0:
            low = before_ref[heads].astype(jnp.bfloat16)
            for c in range(heads):
                high = min((c + 1) * EXTRA, DH)
                out_ref[pl.ds(size, high - c * EXTRA), pl.ds(c * DH, DH)] = low[c * EXTRA:high]


def late_rows(at, queries, locals_, before, heads, embed, tokens, last):
    count = len(queries)
    size, span = locals_[0].shape
    rows, steps = size, 1
    in_specs, operands = [], []
    for n in range(count):
        whole = pl.BlockSpec((rows, span), lambda i, s: (i, 0))
        if isinstance(queries[n], tuple):
            array, side = queries[n]
            per = array.shape[0] // 4 // rows
            in_specs += [pl.BlockSpec((rows, span), lambda i, s, side=side: ((s[0] ^ side) * per, 0)), whole]
            operands += [array, locals_[n]]
        else:
            in_specs += [whole, whole]
            operands += [queries[n], locals_[n]]
    state = pl.BlockSpec(before.shape, lambda i, s: (0, 0, 0))
    in_specs.append(state)
    operands.append(before)
    bit, out_specs, out_shape = None, [], []
    if last is not None:
        mine, bit, got = last
        in_specs += [pl.BlockSpec(memory_space=pltpu.SMEM), state]
        operands += [mine, got]
        out_specs, out_shape = [state], [jax.ShapeDtypeStruct(before.shape, jnp.float32)]
    in_specs += [pl.BlockSpec(memory_space=pl.ANY)] * len(tokens)
    more = EXTRA if embed else 0
    return pl.pallas_call(
        functools.partial(late_kernel, count, heads, embed, bit),
        grid_spec=pltpu.PrefetchScalarGridSpec(
            num_scalar_prefetch=1,
            grid=(steps,),
            in_specs=in_specs,
            out_specs=[
                pl.BlockSpec((rows + (more if n == 0 else 0), span), lambda i, s: (i, 0)) for n in range(count)
            ] + out_specs,
        ),
        out_shape=[
            jax.ShapeDtypeStruct((size + (more if n == 0 else 0), span), jnp.bfloat16) for n in range(count)
        ] + out_shape,
        compiler_params=params(),
        cost_estimate=COST,
        name="late_rows",
    )(at, *operands, *tokens)


def early_out_kernel(*refs):
    ins, outs = refs[:-2], refs[-2:]
    for side in range(2):
        low_ref, high_ref, q_ref, b_ref = ins[side::2]
        out_ref = outs[side]
        parts = []
        for c in range(b_ref.shape[1] // DH):
            high = min((c + 1) * EXTRA, DH)
            parts.append(b_ref[pl.ds(b_ref.shape[0] - EXTRA, high - c * EXTRA), pl.ds(c * DH, DH)])
        state = jnp.concatenate(parts, axis=0)
        size, held, first = out_ref.shape[0], q_ref.shape[0], low_ref.shape[0]
        query = jnp.concatenate([q_ref[...], high_ref[pl.ds(size - first, size - held), :]], axis=0)
        late = jnp.dot(query, state, preferred_element_type=jnp.float32)
        low = low_ref[...].astype(jnp.float32) + late[:first]
        out_ref[pl.ds(0, first), :] = low.astype(jnp.bfloat16)
        high = high_ref[pl.ds(0, size - first), :].astype(jnp.float32) + late[first:]
        out_ref[pl.ds(first, size - first), :] = high.astype(jnp.bfloat16)


def early_out(size, low, high, query, states):
    def full(array):
        return pl.BlockSpec(array.shape, lambda n: (0, 0))

    out = jax.ShapeDtypeStruct((size, DH), jnp.bfloat16)
    operands = [*low, *high, *query, *states]
    return pl.pallas_call(
        early_out_kernel,
        grid=(1,),
        in_specs=[full(y) for y in operands],
        out_specs=[pl.BlockSpec((size, DH), lambda n: (0, 0))] * 2,
        out_shape=[out, out],
        compiler_params=params(),
        cost_estimate=COST,
        name="early_out",
    )(*operands)


def gather_kernel(own_ref, mate_ref, o2_ref, o3_ref, out_ref):
    first = 0
    for ref in (own_ref, mate_ref, o2_ref, o3_ref):
        out_ref[:, pl.ds(first, ref.shape[1])] = ref[...]
        first += ref.shape[1]


def gather_rows(size, *pairs):
    def at(pair):
        index = pair[1] // size
        return pl.BlockSpec((size, pair[0].shape[1]), lambda n: (index, 0))

    width = sum(pair[0].shape[1] for pair in pairs)
    return pl.pallas_call(
        gather_kernel,
        grid=(1,),
        in_specs=[at(pair) for pair in pairs],
        out_specs=pl.BlockSpec((size, width), lambda n: (0, 0)),
        out_shape=jax.ShapeDtypeStruct((size, width), jnp.bfloat16),
        compiler_params=params(),
        cost_estimate=COST,
        name="gather_rows",
    )(*[pair[0] for pair in pairs])


def norm_last(head, gain, share, row, near, x2, x3, out):
    size, narrow = x2.shape
    width = narrow + DH
    index = row // size
    vmem = pl.BlockSpec(memory_space=pltpu.VMEM)

    def kernel(head_ref, gain_ref, near_ref, x2_ref, x3_ref, old_ref, out_ref):
        cut = [0, width, 2 * width, 2 * width + DH, 2 * width + 2 * DH]
        refs = [near_ref.at[:, pl.ds(a, b - a)] for a, b in zip(cut, cut[1:])]
        norm_kernel(head_ref, gain_ref, refs[0], refs[1], x2_ref, x3_ref, refs[2], refs[3], out_ref)

    return pl.pallas_call(
        kernel,
        grid_spec=pltpu.PrefetchScalarGridSpec(
            num_scalar_prefetch=1,
            grid=(1,),
            in_specs=[vmem] * 4 + [pl.BlockSpec(memory_space=pl.ANY)],
            out_specs=pl.BlockSpec((size, 4 * width), lambda n, s: (index, 0)),
        ),
        out_shape=jax.ShapeDtypeStruct((share, 4 * width), jnp.bfloat16),
        input_output_aliases={5: 0},
        compiler_params=params(),
        cost_estimate=COST,
        name="norm_last",
    )(head, gain, near, x2, x3, out)


def norm_kernel(head_ref, gain_ref, own_ref, mate_ref, x2_ref, x3_ref, o2_ref, o3_ref, *rest):
    out_ref = rest[-1]
    head = head_ref[0]
    width = own_ref.shape[1]
    pieces = (
        (own_ref, 0, 0), (mate_ref, 1, 0), (x2_ref, 2, 0), (o2_ref, 2, width - DH), (x3_ref, 3, 0),
        (o3_ref, 3, width - DH),
    )
    total = jnp.zeros((own_ref.shape[0], DH), jnp.float32)
    for ref, _, _ in pieces:
        for c in range(ref.shape[1] // DH):
            wide = ref[:, pl.ds(c * DH, DH)].astype(jnp.float32)
            total += wide * wide
    total = jnp.sum(total, axis=-1, keepdims=True)
    scale = lax.rsqrt(total / (4 * width) + EPS)
    for ref, partner, offset in pieces:
        at = pl.multiple_of((head ^ partner) * width + offset, DH)
        cols = pl.ds(at, ref.shape[1])
        out_ref[:, cols] = (ref[...].astype(jnp.float32) * scale * gain_ref[:, cols]).astype(jnp.bfloat16)


def norm_rows(head, gain, share, row, size, own, mate, x2, x3, o2, o3, out):
    def at(pair, cols):
        index = pair[1] // TILE
        return pl.BlockSpec((TILE, cols), lambda n, s: (index + n, 0))

    width = own[0].shape[1]
    in_specs = [pl.BlockSpec(gain.shape, lambda n, s: (0, 0)), at(own, width), at(mate, width)]
    in_specs += [at(x2, width - DH), at(x3, width - DH), at(o2, DH), at(o3, DH)]
    operands = [gain, own[0], mate[0], x2[0], x3[0], o2[0], o3[0]]
    aliases = {}
    if out is not None:
        in_specs.append(pl.BlockSpec(memory_space=pl.ANY))
        operands.append(out)
        aliases = {len(operands): 0}
    index = row // TILE
    return pl.pallas_call(
        norm_kernel,
        grid_spec=pltpu.PrefetchScalarGridSpec(
            num_scalar_prefetch=1,
            grid=(size // TILE,),
            in_specs=in_specs,
            out_specs=pl.BlockSpec((TILE, 4 * width), lambda n, s: (index + n, 0)),
        ),
        out_shape=jax.ShapeDtypeStruct((share, 4 * width), jnp.bfloat16),
        input_output_aliases=aliases,
        compiler_params=params(),
        cost_estimate=COST,
        name="norm_rows",
    )(head, *operands)


def add_kernel(bit, with_before, mine_ref, total_ref, got_ref, *rest):
    group_ref, after_ref = rest[-2:]
    got = got_ref[...].astype(jnp.float32)
    late = jnp.where((mine_ref[0] & bit) > 0, got, 0.0)
    if with_before:
        late = late + rest[0][...]
    after_ref[...] = late
    group_ref[...] = (total_ref[...].astype(jnp.float32) + got).astype(jnp.bfloat16)


def add_step(mine, bit, total, got, before, tokens):
    vmem = pl.BlockSpec(memory_space=pltpu.VMEM)
    states = [total, got] + ([] if before is None else [before])
    return pl.pallas_call(
        functools.partial(add_kernel, bit, before is not None),
        in_specs=[pl.BlockSpec(memory_space=pltpu.SMEM)] + [vmem] * len(states)
        + [pl.BlockSpec(memory_space=pl.ANY)] * len(tokens),
        out_specs=[vmem, vmem],
        out_shape=[
            jax.ShapeDtypeStruct(total.shape, jnp.bfloat16),
            jax.ShapeDtypeStruct(total.shape, jnp.float32),
        ],
        compiler_params=params(),
        cost_estimate=COST,
        name="add_step",
    )(mine, *states, *tokens)


def swap(x, axis, size, bit):
    return lax.ppermute(x, axis, [(i, i ^ bit) for i in range(size)])


def across(pair):
    return [swap(x, "head", 4, k) for x, k in zip(pair, (2, 3))]


def shards(seq_size, queries, keys, values, norm_gain):
    rows, width = queries.shape
    heads = width // DH
    share = rows // 4
    head = lax.axis_index("head")
    at = jnp.full((1,), head, jnp.int32)
    mine = jnp.full((1,), lax.axis_index("seq"), jnp.int32)
    gain = norm_gain.reshape(1, -1)
    far = (2, 3)

    tail = HALF
    slices = [lax.dynamic_slice(queries, ((head ^ k) * share, width - DH), (share - tail, DH)) for k in far]
    early_q = across(slices)
    within, total = block_states(keys, values, *slices)
    arrays = (queries, keys, values, within)
    group, before, bit, step = total, None, 1, 0
    early_l = []
    while bit < seq_size:
        got = swap(group, "seq", seq_size, bit)
        tokens = []
        if step < 2:
            early = early_rows(at, queries, keys, values, within, step, tail * step, [group])
            early_l.append(across(early))
            tokens = [*early, *(early_q if step == 0 else early_l[0])]
        elif step == 2:
            first = attention_rows(
                arrays, None, at, far, BLK, HALF, 0, heads - 1, jnp.float32, [group], keep=True
            )
            second = attention_rows(arrays, None, at, far, 0, BLK, 0, heads - 1, jnp.bfloat16, first)
            tokens = [*first, *second]
        if bit * 2 < seq_size:
            group, before = add_step(mine, bit, group, got, before, tokens)
        bit, step = bit * 2, step + 1

    def far_rows(start, size, tokens, cost=None, cut=1):
        return attention_rows(arrays, before, at, far, start, size, 0, heads - 1, jnp.bfloat16, tokens, cost, cut)

    *one, before = late_rows(
        at, first[2:], first[:2], before, heads - 1, True, [*early_l[1], *second], (mine, bit // 2, got)
    )
    x1 = across(one)
    two = late_rows(at, [(queries, k) for k in far], second, before, heads - 1, False, one, None)
    x2 = across(two)
    mate = attention_quarter(arrays, before, at, 1, jnp.bfloat16, two)
    mated = swap(mate, "head", 4, 1)
    own = attention_quarter(arrays, before, at, 0, jnp.bfloat16, [mate])
    three = far_rows(BLK + HALF, HALF, [own, *x1], LONG, 2)
    x3, x4 = across(three[0::2]), across(three[1::2])
    state = lax.slice(x1[0], (HALF, 0), (HALF + EXTRA, x1[0].shape[1]))
    other = swap(state, "head", 4, 1)
    o2, o3 = early_out(share, *early_l, early_q, [state, other])
    out = None
    end = share - HALF // 2
    for row, size, (y2, y3) in ((BLK, HALF, x1), (0, BLK, x2), (BLK + HALF, HALF // 2, x3)):
        out = norm_rows(
            at, gain, share, row, size, (own, row), (mated, row), (y2, 0), (y3, 0), (o2, row), (o3, row), out
        )
    near = gather_rows(share - end, (own, end), (mated, end), (o2, end), (o3, end))
    return norm_last(at, gain, share, end, near, x4[0], x4[1], out)


def solution(mesh):
    seq_size = mesh.shape["seq"]

    def body(queries, keys, values, norm_gain):
        return shards(seq_size, queries, keys, values, norm_gain)

    return jax.shard_map(
        body,
        mesh=mesh,
        in_specs=(P("seq", "head"), P("seq", "head"), P("seq", "head"), P()),
        out_specs=P(("seq", "head"), None),
        check_vma=False,
    )
```

```python
import functools

import jax
import jax.numpy as jnp
from jax import lax
from jax.experimental import pallas as pl
from jax.experimental.pallas import tpu as pltpu
from jax.sharding import PartitionSpec as P

DH = 128
BLK = 512
HALF = 256
EXTRA = 48
TILE = 128
EPS = 1e-06
COST = pl.CostEstimate(flops=1024, bytes_accessed=1024, transcendentals=0)
LONG = pl.CostEstimate(flops=10**12, bytes_accessed=1024, transcendentals=0)


def params(mib=49):
    return pltpu.CompilerParams(vmem_limit_bytes=mib * 1024 * 1024)


def state_kernel(parts, tokens, k_ref, v_ref, *rest):
    within_ref, total_ref, k_buf, v_buf, k_sem, v_sem = rest[tokens:]
    rows, width = k_buf.shape
    heads, part = width // DH, rows // parts
    copies = []
    for p in range(parts):
        at = pl.ds(p * part, part)
        pair = (
            pltpu.make_async_copy(k_ref.at[at], k_buf.at[at], k_sem.at[p]),
            pltpu.make_async_copy(v_ref.at[at], v_buf.at[at], v_sem.at[p]),
        )
        for copy in pair:
            copy.start()
        copies.append(pair)
    acc = [jnp.zeros((DH, DH), jnp.float32) for _ in range(heads)]
    for p in range(parts):
        for copy in copies[p]:
            copy.wait()
        for n in range(p * part // BLK, (p + 1) * part // BLK):
            at = pl.ds(n * BLK, BLK)
            for h in range(heads):
                cols = pl.ds(h * DH, DH)
                within_ref[n, h] = acc[h].astype(jnp.bfloat16)
                acc[h] = acc[h] + lax.dot_general(
                    k_buf[at, cols], v_buf[at, cols], (((0,), (0,)), ((), ())),
                    preferred_element_type=jnp.float32,
                )
    for h in range(heads):
        total_ref[h] = acc[h].astype(jnp.bfloat16)


def block_states(keys, values, *tokens):
    rows, width = keys.shape
    heads, blocks = width // DH, rows // BLK
    parts = 4 if blocks % 4 == 0 else 1
    anywhere = pl.BlockSpec(memory_space=pl.ANY)
    vmem = pl.BlockSpec(memory_space=pltpu.VMEM)
    return pl.pallas_call(
        functools.partial(state_kernel, parts, len(tokens)),
        in_specs=[anywhere, anywhere] + [anywhere] * len(tokens),
        out_specs=[vmem, vmem],
        out_shape=[
            jax.ShapeDtypeStruct((blocks, heads, DH, DH), jnp.bfloat16),
            jax.ShapeDtypeStruct((heads, DH, DH), jnp.bfloat16),
        ],
        scratch_shapes=[
            pltpu.VMEM((rows, width), jnp.bfloat16),
            pltpu.VMEM((rows, width), jnp.bfloat16),
            pltpu.SemaphoreType.DMA((parts,)),
            pltpu.SemaphoreType.DMA((parts,)),
        ],
        compiler_params=params(),
        cost_estimate=COST,
        name="block_states",
    )(keys, values, *tokens)


def attend(first, halves, heads, q_ref, k_ref, v_ref, within_ref, before_ref, *out_refs):
    row = lax.broadcasted_iota(jnp.int32, (HALF, HALF), 0)
    col = lax.broadcasted_iota(jnp.int32, (HALF, HALF), 1)
    for h in range(heads):
        cols = pl.ds(h * DH, DH)
        state = within_ref[0, h]
        if before_ref is not None:
            state = state.astype(jnp.float32) + before_ref[h]
        q = q_ref[:, cols]
        out = jnp.dot(q, state.astype(jnp.bfloat16), preferred_element_type=jnp.float32)
        outs = [out[i * HALF:(i + 1) * HALF] for i in range(halves)]
        for j in range(first + halves):
            start = max(j - first, 0)
            there = pl.ds(j * HALF, HALF)
            scores = lax.dot_general(
                q[start * HALF:], k_ref[there, cols], (((1,), (1,)), ((), ())),
                preferred_element_type=jnp.float32,
            )
            low = []
            for i in range(start, halves):
                piece = scores[(i - start) * HALF:(i - start + 1) * HALF]
                if first + i == j:
                    piece = jnp.where(row >= col, piece, 0.0)
                low.append(piece.astype(jnp.bfloat16))
            low = jnp.concatenate(low, axis=0) if len(low) > 1 else low[0]
            more = jnp.dot(low, v_ref[there, cols], preferred_element_type=jnp.float32)
            for i in range(start, halves):
                outs[i] = outs[i] + more[(i - start) * HALF:(i - start + 1) * HALF]
        for i in range(halves):
            part = HALF if len(out_refs) == 1 else HALF * halves // len(out_refs)
            for r in range(0, HALF, part):
                out_ref = out_refs[0] if len(out_refs) == 1 else out_refs[(i * HALF + r) // part]
                low_row = i * HALF if len(out_refs) == 1 else 0
                out_ref[pl.ds(low_row, part), cols] = outs[i][r:r + part].astype(out_ref.dtype)


def attention_rows(arrays, before, at, sides, start, size, head, heads, kind, tokens, cost=None, cut=1, keep=False):
    queries, keys, values, within = arrays
    rows, width = queries.shape
    share = rows // 4
    halves = size // HALF
    first = (start % BLK) // HALF
    k_rows = BLK if first + halves > 1 else HALF
    span = heads * DH
    across = head // heads
    count = len(sides)

    def quarter(n, s):
        side = sides[0]
        for i in range(1, count):
            side = jnp.where(n == i, sides[i], side)
        return s[0] ^ side

    def block(n, s):
        return quarter(n, s) * (share // BLK) + start // BLK

    keys_spec = pl.BlockSpec((k_rows, span), lambda n, s: (block(n, s) * (BLK // k_rows), across))
    in_specs = [
        pl.BlockSpec((size, span), lambda n, s: (quarter(n, s) * (share // size) + start // size, across)),
        keys_spec,
        keys_spec,
        pl.BlockSpec((1, heads, DH, DH), lambda n, s: (block(n, s), across, 0, 0)),
    ]
    operands = [queries, keys, values, within]
    if before is not None:
        in_specs.append(pl.BlockSpec(before.shape, lambda n, s: (0, 0, 0)))
        operands.append(before)
    in_specs += [pl.BlockSpec(memory_space=pl.ANY)] * len(tokens)

    def kernel(ids_ref, q_ref, k_ref, v_ref, within_ref, *rest):
        before_ref = None if before is None else rest[0]
        outs = rest[len(rest) - count * (cut + keep):]
        for n in range(count):
            @pl.when(pl.program_id(0) == n)
            def _(n=n):
                mine = outs[n * cut:(n + 1) * cut]
                attend(first, halves, heads, q_ref, k_ref, v_ref, within_ref, before_ref, *mine)
                if keep:
                    outs[count * cut + n][...] = q_ref[...]

    return pl.pallas_call(
        kernel,
        grid_spec=pltpu.PrefetchScalarGridSpec(
            num_scalar_prefetch=1,
            grid=(count,),
            in_specs=in_specs,
            out_specs=[pl.BlockSpec((size // cut, span), lambda n, s: (0, 0))] * (count * (cut + keep)),
        ),
        out_shape=[jax.ShapeDtypeStruct((size // cut, span), kind)] * (count * cut)
        + [jax.ShapeDtypeStruct((size, span), jnp.bfloat16)] * (count * keep),
        compiler_params=params(),
        cost_estimate=COST if cost is None else cost,
        name="attention_rows",
    )(at, *operands, *tokens)


def attention_quarter(arrays, before, at, side, kind, tokens):
    queries, keys, values, within = arrays
    rows, width = queries.shape
    share = rows // 4
    heads, blocks = width // DH, share // BLK
    block = pl.BlockSpec((BLK, width), lambda n, s: ((s[0] ^ side) * blocks + n, 0))
    state = pl.BlockSpec((1, heads, DH, DH), lambda n, s: ((s[0] ^ side) * blocks + n, 0, 0, 0))
    in_specs = [block, block, block, state]
    operands = [queries, keys, values, within]
    if before is not None:
        in_specs.append(pl.BlockSpec(before.shape, lambda n, s: (0, 0, 0)))
        operands.append(before)
    in_specs += [pl.BlockSpec(memory_space=pl.ANY)] * len(tokens)

    def kernel(quarter_ref, q_ref, k_ref, v_ref, within_ref, *rest):
        before_ref = None if before is None else rest[0]
        attend(0, BLK // HALF, heads, q_ref, k_ref, v_ref, within_ref, before_ref, rest[-1])

    return pl.pallas_call(
        kernel,
        grid_spec=pltpu.PrefetchScalarGridSpec(
            num_scalar_prefetch=1,
            grid=(blocks,),
            in_specs=in_specs,
            out_specs=pl.BlockSpec((BLK, width), lambda n, s: (n, 0)),
        ),
        out_shape=jax.ShapeDtypeStruct((share, width), kind),
        compiler_params=params(),
        cost_estimate=COST,
        name="attention_quarter",
    )(at, *operands, *tokens)


def early_kernel(tail, head_ref, q_ref, k_ref, v_ref, within_ref, *rest):
    outs = rest[len(rest) - 2:]
    if tail:
        tail_ref = rest[0]
    for side in range(2):
        @pl.when(pl.program_id(0) == side)
        def _(side=side):
            attend(0, BLK // HALF, 1, q_ref, k_ref, v_ref, within_ref, None, outs[side])
            if tail:
                outs[side][pl.ds(BLK, tail), :] = tail_ref[...]


def early_rows(head, queries, keys, values, within, n, tail, tokens):
    rows, width = keys.shape
    share, last = rows // 4, width // DH - 1
    blocks = share // BLK
    block = pl.BlockSpec((BLK, DH), lambda i, s: ((s[0] ^ (2 + i)) * blocks + n, last))
    in_specs = [
        block, block, block, pl.BlockSpec((1, 1, DH, DH), lambda i, s: ((s[0] ^ (2 + i)) * blocks + n, last, 0, 0)),
    ]
    operands = [queries, keys, values, within]
    if tail:
        per = share // tail
        in_specs.append(pl.BlockSpec((tail, DH), lambda i, s: ((s[0] ^ (2 + i)) * per + per - 1, last)))
        operands.append(queries)
    in_specs += [pl.BlockSpec(memory_space=pl.ANY)] * len(tokens)
    return pl.pallas_call(
        functools.partial(early_kernel, tail),
        grid_spec=pltpu.PrefetchScalarGridSpec(
            num_scalar_prefetch=1,
            grid=(2,),
            in_specs=in_specs,
            out_specs=[pl.BlockSpec((BLK + tail, DH), lambda i, s: (0, 0))] * 2,
        ),
        out_shape=[jax.ShapeDtypeStruct((BLK + tail, DH), jnp.bfloat16)] * 2,
        compiler_params=params(),
        cost_estimate=COST,
        name="early_rows",
    )(head, *operands, *tokens)


def late_kernel(count, heads, embed, bit, head_ref, *refs):
    before_ref = refs[2 * count]
    outs = refs[len(refs) - count:]
    if bit is not None:
        mine_ref, got_ref = refs[2 * count + 1:2 * count + 3]
        outs, after_ref = refs[len(refs) - count - 1:-1], refs[-1]
        after_ref[...] = before_ref[...] + jnp.where((mine_ref[0] & bit) > 0, got_ref[...].astype(jnp.float32), 0.0)
        before_ref = after_ref
    for n in range(count):
        q_ref, local_ref, out_ref = refs[2 * n], refs[2 * n + 1], outs[n]
        size = q_ref.shape[0]
        for h in range(heads):
            cols = pl.ds(h * DH, DH)
            out = local_ref[:, cols].astype(jnp.float32) + jnp.dot(
                q_ref[:, cols], before_ref[h].astype(jnp.bfloat16), preferred_element_type=jnp.float32
            )
            out_ref[pl.ds(0, size), cols] = out.astype(jnp.bfloat16)
        if embed and n == 0:
            low = before_ref[heads].astype(jnp.bfloat16)
            for c in range(heads):
                high = min((c + 1) * EXTRA, DH)
                out_ref[pl.ds(size, high - c * EXTRA), pl.ds(c * DH, DH)] = low[c * EXTRA:high]


def late_rows(at, queries, locals_, before, heads, embed, tokens, last):
    count = len(queries)
    size, span = locals_[0].shape
    rows, steps = size, 1
    in_specs, operands = [], []
    for n in range(count):
        whole = pl.BlockSpec((rows, span), lambda i, s: (i, 0))
        if isinstance(queries[n], tuple):
            array, side = queries[n]
            per = array.shape[0] // 4 // rows
            in_specs += [pl.BlockSpec((rows, span), lambda i, s, side=side: ((s[0] ^ side) * per, 0)), whole]
            operands += [array, locals_[n]]
        else:
            in_specs += [whole, whole]
            operands += [queries[n], locals_[n]]
    state = pl.BlockSpec(before.shape, lambda i, s: (0, 0, 0))
    in_specs.append(state)
    operands.append(before)
    bit, out_specs, out_shape = None, [], []
    if last is not None:
        mine, bit, got = last
        in_specs += [pl.BlockSpec(memory_space=pltpu.SMEM), state]
        operands += [mine, got]
        out_specs, out_shape = [state], [jax.ShapeDtypeStruct(before.shape, jnp.float32)]
    in_specs += [pl.BlockSpec(memory_space=pl.ANY)] * len(tokens)
    more = EXTRA if embed else 0
    return pl.pallas_call(
        functools.partial(late_kernel, count, heads, embed, bit),
        grid_spec=pltpu.PrefetchScalarGridSpec(
            num_scalar_prefetch=1,
            grid=(steps,),
            in_specs=in_specs,
            out_specs=[
                pl.BlockSpec((rows + (more if n == 0 else 0), span), lambda i, s: (i, 0)) for n in range(count)
            ] + out_specs,
        ),
        out_shape=[
            jax.ShapeDtypeStruct((size + (more if n == 0 else 0), span), jnp.bfloat16) for n in range(count)
        ] + out_shape,
        compiler_params=params(),
        cost_estimate=COST,
        name="late_rows",
    )(at, *operands, *tokens)


def early_out_kernel(*refs):
    ins, outs = refs[:-2], refs[-2:]
    for side in range(2):
        low_ref, high_ref, q_ref, b_ref = ins[side::2]
        out_ref = outs[side]
        parts = []
        for c in range(b_ref.shape[1] // DH):
            high = min((c + 1) * EXTRA, DH)
            parts.append(b_ref[pl.ds(b_ref.shape[0] - EXTRA, high - c * EXTRA), pl.ds(c * DH, DH)])
        state = jnp.concatenate(parts, axis=0)
        size, held, first = out_ref.shape[0], q_ref.shape[0], low_ref.shape[0]
        query = jnp.concatenate([q_ref[...], high_ref[pl.ds(size - first, size - held), :]], axis=0)
        late = jnp.dot(query, state, preferred_element_type=jnp.float32)
        low = low_ref[...].astype(jnp.float32) + late[:first]
        out_ref[pl.ds(0, first), :] = low.astype(jnp.bfloat16)
        high = high_ref[pl.ds(0, size - first), :].astype(jnp.float32) + late[first:]
        out_ref[pl.ds(first, size - first), :] = high.astype(jnp.bfloat16)


def early_out(size, low, high, query, states):
    def full(array):
        return pl.BlockSpec(array.shape, lambda n: (0, 0))

    out = jax.ShapeDtypeStruct((size, DH), jnp.bfloat16)
    operands = [*low, *high, *query, *states]
    return pl.pallas_call(
        early_out_kernel,
        grid=(1,),
        in_specs=[full(y) for y in operands],
        out_specs=[pl.BlockSpec((size, DH), lambda n: (0, 0))] * 2,
        out_shape=[out, out],
        compiler_params=params(),
        cost_estimate=COST,
        name="early_out",
    )(*operands)


def gather_kernel(own_ref, mate_ref, o2_ref, o3_ref, out_ref):
    first = 0
    for ref in (own_ref, mate_ref, o2_ref, o3_ref):
        out_ref[:, pl.ds(first, ref.shape[1])] = ref[...]
        first += ref.shape[1]


def gather_rows(size, *pairs):
    def at(pair):
        index = pair[1] // size
        return pl.BlockSpec((size, pair[0].shape[1]), lambda n: (index, 0))

    width = sum(pair[0].shape[1] for pair in pairs)
    return pl.pallas_call(
        gather_kernel,
        grid=(1,),
        in_specs=[at(pair) for pair in pairs],
        out_specs=pl.BlockSpec((size, width), lambda n: (0, 0)),
        out_shape=jax.ShapeDtypeStruct((size, width), jnp.bfloat16),
        compiler_params=params(),
        cost_estimate=COST,
        name="gather_rows",
    )(*[pair[0] for pair in pairs])


def norm_last(head, gain, share, row, near, x2, x3, out):
    size, narrow = x2.shape
    width = narrow + DH
    index = row // size
    vmem = pl.BlockSpec(memory_space=pltpu.VMEM)

    def kernel(head_ref, gain_ref, near_ref, x2_ref, x3_ref, old_ref, out_ref):
        cut = [0, width, 2 * width, 2 * width + DH, 2 * width + 2 * DH]
        refs = [near_ref.at[:, pl.ds(a, b - a)] for a, b in zip(cut, cut[1:])]
        norm_kernel(head_ref, gain_ref, refs[0], refs[1], x2_ref, x3_ref, refs[2], refs[3], out_ref)

    return pl.pallas_call(
        kernel,
        grid_spec=pltpu.PrefetchScalarGridSpec(
            num_scalar_prefetch=1,
            grid=(1,),
            in_specs=[vmem] * 4 + [pl.BlockSpec(memory_space=pl.ANY)],
            out_specs=pl.BlockSpec((size, 4 * width), lambda n, s: (index, 0)),
        ),
        out_shape=jax.ShapeDtypeStruct((share, 4 * width), jnp.bfloat16),
        input_output_aliases={5: 0},
        compiler_params=params(),
        cost_estimate=COST,
        name="norm_last",
    )(head, gain, near, x2, x3, out)


def norm_kernel(head_ref, gain_ref, own_ref, mate_ref, x2_ref, x3_ref, o2_ref, o3_ref, *rest):
    out_ref = rest[-1]
    head = head_ref[0]
    width = own_ref.shape[1]
    pieces = (
        (own_ref, 0, 0), (mate_ref, 1, 0), (x2_ref, 2, 0), (o2_ref, 2, width - DH), (x3_ref, 3, 0),
        (o3_ref, 3, width - DH),
    )
    total = jnp.zeros((own_ref.shape[0], DH), jnp.float32)
    for ref, _, _ in pieces:
        for c in range(ref.shape[1] // DH):
            wide = ref[:, pl.ds(c * DH, DH)].astype(jnp.float32)
            total += wide * wide
    total = jnp.sum(total, axis=-1, keepdims=True)
    scale = lax.rsqrt(total / (4 * width) + EPS)
    for ref, partner, offset in pieces:
        at = pl.multiple_of((head ^ partner) * width + offset, DH)
        cols = pl.ds(at, ref.shape[1])
        out_ref[:, cols] = (ref[...].astype(jnp.float32) * scale * gain_ref[:, cols]).astype(jnp.bfloat16)


def norm_rows(head, gain, share, row, size, own, mate, x2, x3, o2, o3, out):
    def at(pair, cols):
        index = pair[1] // TILE
        return pl.BlockSpec((TILE, cols), lambda n, s: (index + n, 0))

    width = own[0].shape[1]
    in_specs = [pl.BlockSpec(gain.shape, lambda n, s: (0, 0)), at(own, width), at(mate, width)]
    in_specs += [at(x2, width - DH), at(x3, width - DH), at(o2, DH), at(o3, DH)]
    operands = [gain, own[0], mate[0], x2[0], x3[0], o2[0], o3[0]]
    aliases = {}
    if out is not None:
        in_specs.append(pl.BlockSpec(memory_space=pl.ANY))
        operands.append(out)
        aliases = {len(operands): 0}
    index = row // TILE
    return pl.pallas_call(
        norm_kernel,
        grid_spec=pltpu.PrefetchScalarGridSpec(
            num_scalar_prefetch=1,
            grid=(size // TILE,),
            in_specs=in_specs,
            out_specs=pl.BlockSpec((TILE, 4 * width), lambda n, s: (index + n, 0)),
        ),
        out_shape=jax.ShapeDtypeStruct((share, 4 * width), jnp.bfloat16),
        input_output_aliases=aliases,
        compiler_params=params(),
        cost_estimate=COST,
        name="norm_rows",
    )(head, *operands)


def norm_block_kernel(row, size, places, width, head_ref, *refs):
    count, tiles = len(places), size // TILE
    ins = refs[:count + 1]
    out_ref, gain_buf, *bufs, out_buf, gain_sem, in_sem, out_sem = refs[len(refs) - count - 6:]
    gain_copy = pltpu.make_async_copy(ins[0], gain_buf, gain_sem)
    gain_copy.start()
    copies = []
    for t in range(tiles):
        here = pl.ds(t * TILE, TILE)
        copies.append([])
        for n in range(count):
            there = pl.ds(places[n][0] + t * TILE, TILE)
            copy = pltpu.make_async_copy(ins[n + 1].at[there], bufs[n].at[here], in_sem.at[t, n])
            copy.start()
            copies[t].append(copy)
    gain_copy.wait()
    head = head_ref[0]
    sent = []
    for t in range(tiles):
        here = pl.ds(t * TILE, TILE)
        for copy in copies[t]:
            copy.wait()
        total = jnp.zeros((TILE, DH), jnp.float32)
        for buf in bufs:
            for c in range(buf.shape[1] // DH):
                wide = buf[here, pl.ds(c * DH, DH)].astype(jnp.float32)
                total += wide * wide
        scale = lax.rsqrt(jnp.sum(total, axis=-1, keepdims=True) / (4 * width) + EPS)
        for buf, (_, partner, offset) in zip(bufs, places):
            at = pl.multiple_of((head ^ partner) * width + offset, DH)
            cols = pl.ds(at, buf.shape[1])
            out_buf[here, cols] = (buf[here, :].astype(jnp.float32) * scale * gain_buf[:, cols]).astype(jnp.bfloat16)
        copy = pltpu.make_async_copy(out_buf.at[here], out_ref.at[pl.ds(row + t * TILE, TILE)], out_sem.at[t])
        copy.start()
        sent.append(copy)
    for copy in sent:
        copy.wait()


def norm_block(head, gain, share, row, size, own, mate, x2, x3, o2, o3, out):
    width = own[0].shape[1]
    pieces = ((own, 0, 0), (mate, 1, 0), (x2, 2, 0), (o2, 2, width - DH), (x3, 3, 0), (o3, 3, width - DH))
    arrays = [piece[0][0] for piece in pieces]
    places = [(piece[0][1], piece[1], piece[2]) for piece in pieces]
    anywhere = pl.BlockSpec(memory_space=pl.ANY)
    operands = [gain, *arrays] + ([] if out is None else [out])
    tiles = size // TILE
    return pl.pallas_call(
        functools.partial(norm_block_kernel, row, size, places, width),
        in_specs=[pl.BlockSpec(memory_space=pltpu.SMEM)] + [anywhere] * len(operands),
        out_specs=anywhere,
        out_shape=jax.ShapeDtypeStruct((share, 4 * width), jnp.bfloat16),
        input_output_aliases={} if out is None else {len(operands): 0},
        scratch_shapes=[pltpu.VMEM(gain.shape, jnp.float32)]
        + [pltpu.VMEM((size, array.shape[1]), jnp.bfloat16) for array in arrays]
        + [
            pltpu.VMEM((size, 4 * width), jnp.bfloat16),
            pltpu.SemaphoreType.DMA(()),
            pltpu.SemaphoreType.DMA((tiles, len(arrays))),
            pltpu.SemaphoreType.DMA((tiles,)),
        ],
        compiler_params=params(),
        cost_estimate=COST,
        name="norm_block",
    )(head, *operands)


def add_kernel(bit, with_before, mine_ref, total_ref, got_ref, *rest):
    group_ref, after_ref = rest[-2:]
    got = got_ref[...].astype(jnp.float32)
    late = jnp.where((mine_ref[0] & bit) > 0, got, 0.0)
    if with_before:
        late = late + rest[0][...]
    after_ref[...] = late
    group_ref[...] = (total_ref[...].astype(jnp.float32) + got).astype(jnp.bfloat16)


def add_step(mine, bit, total, got, before, tokens):
    vmem = pl.BlockSpec(memory_space=pltpu.VMEM)
    states = [total, got] + ([] if before is None else [before])
    return pl.pallas_call(
        functools.partial(add_kernel, bit, before is not None),
        in_specs=[pl.BlockSpec(memory_space=pltpu.SMEM)] + [vmem] * len(states)
        + [pl.BlockSpec(memory_space=pl.ANY)] * len(tokens),
        out_specs=[vmem, vmem],
        out_shape=[
            jax.ShapeDtypeStruct(total.shape, jnp.bfloat16),
            jax.ShapeDtypeStruct(total.shape, jnp.float32),
        ],
        compiler_params=params(),
        cost_estimate=COST,
        name="add_step",
    )(mine, *states, *tokens)


def swap(x, axis, size, bit):
    return lax.ppermute(x, axis, [(i, i ^ bit) for i in range(size)])


def across(pair):
    return [swap(x, "head", 4, k) for x, k in zip(pair, (2, 3))]


def shards(seq_size, queries, keys, values, norm_gain):
    rows, width = queries.shape
    heads = width // DH
    share = rows // 4
    head = lax.axis_index("head")
    at = jnp.full((1,), head, jnp.int32)
    mine = jnp.full((1,), lax.axis_index("seq"), jnp.int32)
    gain = norm_gain.reshape(1, -1)
    far = (2, 3)

    tail = HALF
    slices = [lax.dynamic_slice(queries, ((head ^ k) * share, width - DH), (share - tail, DH)) for k in far]
    early_q = across(slices)
    within, total = block_states(keys, values, *slices)
    arrays = (queries, keys, values, within)
    group, before, bit, step = total, None, 1, 0
    early_l = []
    while bit < seq_size:
        got = swap(group, "seq", seq_size, bit)
        tokens = []
        if step < 2:
            early = early_rows(at, queries, keys, values, within, step, tail * step, [group])
            early_l.append(across(early))
            tokens = [*early, *(early_q if step == 0 else early_l[0])]
        elif step == 2:
            first = attention_rows(
                arrays, None, at, far, BLK, HALF, 0, heads - 1, jnp.float32, [group], keep=True
            )
            second = attention_rows(arrays, None, at, far, 0, BLK, 0, heads - 1, jnp.bfloat16, first)
            tokens = [*first, *second]
        if bit * 2 < seq_size:
            group, before = add_step(mine, bit, group, got, before, tokens)
        bit, step = bit * 2, step + 1

    def far_rows(start, size, tokens, cost=None, cut=1):
        return attention_rows(arrays, before, at, far, start, size, 0, heads - 1, jnp.bfloat16, tokens, cost, cut)

    *one, before = late_rows(
        at, first[2:], first[:2], before, heads - 1, True, [*early_l[1], *second], (mine, bit // 2, got)
    )
    x1 = across(one)
    two = late_rows(at, [(queries, k) for k in far], second, before, heads - 1, False, one, None)
    x2 = across(two)
    mate = attention_quarter(arrays, before, at, 1, jnp.bfloat16, two)
    mated = swap(mate, "head", 4, 1)
    own = attention_quarter(arrays, before, at, 0, jnp.bfloat16, [mate])
    three = far_rows(BLK + HALF, HALF, [own, *x1], LONG, 2)
    x3, x4 = across(three[0::2]), across(three[1::2])
    state = lax.slice(x1[0], (HALF, 0), (HALF + EXTRA, x1[0].shape[1]))
    other = swap(state, "head", 4, 1)
    o2, o3 = early_out(share, *early_l, early_q, [state, other])
    out = None
    end = share - HALF // 2
    for row, size, (y2, y3) in ((BLK, HALF, x1), (0, BLK, x2), (BLK + HALF, HALF // 2, x3)):
        norm = norm_block if size == BLK else norm_rows
        out = norm(
            at, gain, share, row, size, (own, row), (mated, row), (y2, 0), (y3, 0), (o2, row), (o3, row), out
        )
    near = gather_rows(share - end, (own, end), (mated, end), (o2, end), (o3, end))
    return norm_last(at, gain, share, end, near, x4[0], x4[1], out)


def solution(mesh):
    seq_size = mesh.shape["seq"]

    def body(queries, keys, values, norm_gain):
        return shards(seq_size, queries, keys, values, norm_gain)

    return jax.shard_map(
        body,
        mesh=mesh,
        in_specs=(P("seq", "head"), P("seq", "head"), P("seq", "head"), P()),
        out_specs=P(("seq", "head"), None),
        check_vma=False,
    )
```

```python
import functools

import jax
import jax.numpy as jnp
from jax import lax
from jax.experimental import pallas as pl
from jax.experimental.pallas import tpu as pltpu
from jax.sharding import PartitionSpec as P

DH = 128
BLK = 512
HALF = 256
EXTRA = 48
TILE = 128
EPS = 1e-06
COST = pl.CostEstimate(flops=1024, bytes_accessed=1024, transcendentals=0)
LONG = pl.CostEstimate(flops=10**12, bytes_accessed=1024, transcendentals=0)


def params(mib=49):
    return pltpu.CompilerParams(vmem_limit_bytes=mib * 1024 * 1024)


def state_kernel(parts, tokens, k_ref, v_ref, *rest):
    within_ref, total_ref, k_buf, v_buf, k_sem, v_sem = rest[tokens:]
    rows, width = k_buf.shape
    heads, part = width // DH, rows // parts
    copies = []
    for p in range(parts):
        at = pl.ds(p * part, part)
        pair = (
            pltpu.make_async_copy(k_ref.at[at], k_buf.at[at], k_sem.at[p]),
            pltpu.make_async_copy(v_ref.at[at], v_buf.at[at], v_sem.at[p]),
        )
        for copy in pair:
            copy.start()
        copies.append(pair)
    acc = [jnp.zeros((DH, DH), jnp.float32) for _ in range(heads)]
    for p in range(parts):
        for copy in copies[p]:
            copy.wait()
        for n in range(p * part // BLK, (p + 1) * part // BLK):
            at = pl.ds(n * BLK, BLK)
            for h in range(heads):
                cols = pl.ds(h * DH, DH)
                within_ref[n, h] = acc[h].astype(jnp.bfloat16)
                acc[h] = acc[h] + lax.dot_general(
                    k_buf[at, cols], v_buf[at, cols], (((0,), (0,)), ((), ())),
                    preferred_element_type=jnp.float32,
                )
    for h in range(heads):
        total_ref[h] = acc[h].astype(jnp.bfloat16)


def block_states(keys, values, *tokens):
    rows, width = keys.shape
    heads, blocks = width // DH, rows // BLK
    parts = 4 if blocks % 4 == 0 else 1
    anywhere = pl.BlockSpec(memory_space=pl.ANY)
    vmem = pl.BlockSpec(memory_space=pltpu.VMEM)
    return pl.pallas_call(
        functools.partial(state_kernel, parts, len(tokens)),
        in_specs=[anywhere, anywhere] + [anywhere] * len(tokens),
        out_specs=[vmem, vmem],
        out_shape=[
            jax.ShapeDtypeStruct((blocks, heads, DH, DH), jnp.bfloat16),
            jax.ShapeDtypeStruct((heads, DH, DH), jnp.bfloat16),
        ],
        scratch_shapes=[
            pltpu.VMEM((rows, width), jnp.bfloat16),
            pltpu.VMEM((rows, width), jnp.bfloat16),
            pltpu.SemaphoreType.DMA((parts,)),
            pltpu.SemaphoreType.DMA((parts,)),
        ],
        compiler_params=params(),
        cost_estimate=COST,
        name="block_states",
    )(keys, values, *tokens)


def attend(first, halves, heads, q_ref, k_ref, v_ref, within_ref, before_ref, *out_refs):
    row = lax.broadcasted_iota(jnp.int32, (HALF, HALF), 0)
    col = lax.broadcasted_iota(jnp.int32, (HALF, HALF), 1)
    for h in range(heads):
        cols = pl.ds(h * DH, DH)
        state = within_ref[0, h]
        if before_ref is not None:
            state = state.astype(jnp.float32) + before_ref[h]
        q = q_ref[:, cols]
        out = jnp.dot(q, state.astype(jnp.bfloat16), preferred_element_type=jnp.float32)
        outs = [out[i * HALF:(i + 1) * HALF] for i in range(halves)]
        for j in range(first + halves):
            start = max(j - first, 0)
            there = pl.ds(j * HALF, HALF)
            scores = lax.dot_general(
                q[start * HALF:], k_ref[there, cols], (((1,), (1,)), ((), ())),
                preferred_element_type=jnp.float32,
            )
            low = []
            for i in range(start, halves):
                piece = scores[(i - start) * HALF:(i - start + 1) * HALF]
                if first + i == j:
                    piece = jnp.where(row >= col, piece, 0.0)
                low.append(piece.astype(jnp.bfloat16))
            low = jnp.concatenate(low, axis=0) if len(low) > 1 else low[0]
            more = jnp.dot(low, v_ref[there, cols], preferred_element_type=jnp.float32)
            for i in range(start, halves):
                outs[i] = outs[i] + more[(i - start) * HALF:(i - start + 1) * HALF]
        for i in range(halves):
            part = HALF if len(out_refs) == 1 else HALF * halves // len(out_refs)
            for r in range(0, HALF, part):
                out_ref = out_refs[0] if len(out_refs) == 1 else out_refs[(i * HALF + r) // part]
                low_row = i * HALF if len(out_refs) == 1 else 0
                out_ref[pl.ds(low_row, part), cols] = outs[i][r:r + part].astype(out_ref.dtype)


def attention_rows(arrays, before, at, sides, start, size, head, heads, kind, tokens, cost=None, cut=1, keep=False):
    queries, keys, values, within = arrays
    rows, width = queries.shape
    share = rows // 4
    halves = size // HALF
    first = (start % BLK) // HALF
    k_rows = BLK if first + halves > 1 else HALF
    span = heads * DH
    across = head // heads
    count = len(sides)

    def quarter(n, s):
        side = sides[0]
        for i in range(1, count):
            side = jnp.where(n == i, sides[i], side)
        return s[0] ^ side

    def block(n, s):
        return quarter(n, s) * (share // BLK) + start // BLK

    keys_spec = pl.BlockSpec((k_rows, span), lambda n, s: (block(n, s) * (BLK // k_rows), across))
    in_specs = [
        pl.BlockSpec((size, span), lambda n, s: (quarter(n, s) * (share // size) + start // size, across)),
        keys_spec,
        keys_spec,
        pl.BlockSpec((1, heads, DH, DH), lambda n, s: (block(n, s), across, 0, 0)),
    ]
    operands = [queries, keys, values, within]
    if before is not None:
        in_specs.append(pl.BlockSpec(before.shape, lambda n, s: (0, 0, 0)))
        operands.append(before)
    in_specs += [pl.BlockSpec(memory_space=pl.ANY)] * len(tokens)

    def kernel(ids_ref, q_ref, k_ref, v_ref, within_ref, *rest):
        before_ref = None if before is None else rest[0]
        outs = rest[len(rest) - count * (cut + keep):]
        for n in range(count):
            @pl.when(pl.program_id(0) == n)
            def _(n=n):
                mine = outs[n * cut:(n + 1) * cut]
                attend(first, halves, heads, q_ref, k_ref, v_ref, within_ref, before_ref, *mine)
                if keep:
                    outs[count * cut + n][...] = q_ref[...]

    return pl.pallas_call(
        kernel,
        grid_spec=pltpu.PrefetchScalarGridSpec(
            num_scalar_prefetch=1,
            grid=(count,),
            in_specs=in_specs,
            out_specs=[pl.BlockSpec((size // cut, span), lambda n, s: (0, 0))] * (count * (cut + keep)),
        ),
        out_shape=[jax.ShapeDtypeStruct((size // cut, span), kind)] * (count * cut)
        + [jax.ShapeDtypeStruct((size, span), jnp.bfloat16)] * (count * keep),
        compiler_params=params(),
        cost_estimate=COST if cost is None else cost,
        name="attention_rows",
    )(at, *operands, *tokens)


def attention_quarter(arrays, before, at, side, kind, tokens):
    queries, keys, values, within = arrays
    rows, width = queries.shape
    share = rows // 4
    heads, blocks = width // DH, share // BLK
    block = pl.BlockSpec((BLK, width), lambda n, s: ((s[0] ^ side) * blocks + n, 0))
    state = pl.BlockSpec((1, heads, DH, DH), lambda n, s: ((s[0] ^ side) * blocks + n, 0, 0, 0))
    in_specs = [block, block, block, state]
    operands = [queries, keys, values, within]
    if before is not None:
        in_specs.append(pl.BlockSpec(before.shape, lambda n, s: (0, 0, 0)))
        operands.append(before)
    in_specs += [pl.BlockSpec(memory_space=pl.ANY)] * len(tokens)

    def kernel(quarter_ref, q_ref, k_ref, v_ref, within_ref, *rest):
        before_ref = None if before is None else rest[0]
        attend(0, BLK // HALF, heads, q_ref, k_ref, v_ref, within_ref, before_ref, rest[-1])

    return pl.pallas_call(
        kernel,
        grid_spec=pltpu.PrefetchScalarGridSpec(
            num_scalar_prefetch=1,
            grid=(blocks,),
            in_specs=in_specs,
            out_specs=pl.BlockSpec((BLK, width), lambda n, s: (n, 0)),
        ),
        out_shape=jax.ShapeDtypeStruct((share, width), kind),
        compiler_params=params(),
        cost_estimate=COST,
        name="attention_quarter",
    )(at, *operands, *tokens)


def early_kernel(tail, head_ref, q_ref, k_ref, v_ref, within_ref, *rest):
    outs = rest[len(rest) - 2:]
    if tail:
        tail_ref = rest[0]
    for side in range(2):
        @pl.when(pl.program_id(0) == side)
        def _(side=side):
            attend(0, BLK // HALF, 1, q_ref, k_ref, v_ref, within_ref, None, outs[side])
            if tail:
                outs[side][pl.ds(BLK, tail), :] = tail_ref[...]


def early_rows(head, queries, keys, values, within, n, tail, tokens):
    rows, width = keys.shape
    share, last = rows // 4, width // DH - 1
    blocks = share // BLK
    block = pl.BlockSpec((BLK, DH), lambda i, s: ((s[0] ^ (2 + i)) * blocks + n, last))
    in_specs = [
        block, block, block, pl.BlockSpec((1, 1, DH, DH), lambda i, s: ((s[0] ^ (2 + i)) * blocks + n, last, 0, 0)),
    ]
    operands = [queries, keys, values, within]
    if tail:
        per = share // tail
        in_specs.append(pl.BlockSpec((tail, DH), lambda i, s: ((s[0] ^ (2 + i)) * per + per - 1, last)))
        operands.append(queries)
    in_specs += [pl.BlockSpec(memory_space=pl.ANY)] * len(tokens)
    return pl.pallas_call(
        functools.partial(early_kernel, tail),
        grid_spec=pltpu.PrefetchScalarGridSpec(
            num_scalar_prefetch=1,
            grid=(2,),
            in_specs=in_specs,
            out_specs=[pl.BlockSpec((BLK + tail, DH), lambda i, s: (0, 0))] * 2,
        ),
        out_shape=[jax.ShapeDtypeStruct((BLK + tail, DH), jnp.bfloat16)] * 2,
        compiler_params=params(),
        cost_estimate=COST,
        name="early_rows",
    )(head, *operands, *tokens)


def late_kernel(count, heads, embed, bit, head_ref, *refs):
    before_ref = refs[2 * count]
    outs = refs[len(refs) - count:]
    if bit is not None:
        mine_ref, got_ref = refs[2 * count + 1:2 * count + 3]
        outs, after_ref = refs[len(refs) - count - 1:-1], refs[-1]
        after_ref[...] = before_ref[...] + jnp.where((mine_ref[0] & bit) > 0, got_ref[...].astype(jnp.float32), 0.0)
        before_ref = after_ref
    for n in range(count):
        q_ref, local_ref, out_ref = refs[2 * n], refs[2 * n + 1], outs[n]
        size = q_ref.shape[0]
        for h in range(heads):
            cols = pl.ds(h * DH, DH)
            out = local_ref[:, cols].astype(jnp.float32) + jnp.dot(
                q_ref[:, cols], before_ref[h].astype(jnp.bfloat16), preferred_element_type=jnp.float32
            )
            out_ref[pl.ds(0, size), cols] = out.astype(jnp.bfloat16)
        if embed and n == 0:
            low = before_ref[heads].astype(jnp.bfloat16)
            for c in range(heads):
                high = min((c + 1) * EXTRA, DH)
                out_ref[pl.ds(size, high - c * EXTRA), pl.ds(c * DH, DH)] = low[c * EXTRA:high]


def late_rows(at, queries, locals_, before, heads, embed, tokens, last):
    count = len(queries)
    size, span = locals_[0].shape
    rows, steps = size, 1
    in_specs, operands = [], []
    for n in range(count):
        whole = pl.BlockSpec((rows, span), lambda i, s: (i, 0))
        if isinstance(queries[n], tuple):
            array, side = queries[n]
            per = array.shape[0] // 4 // rows
            in_specs += [pl.BlockSpec((rows, span), lambda i, s, side=side: ((s[0] ^ side) * per, 0)), whole]
            operands += [array, locals_[n]]
        else:
            in_specs += [whole, whole]
            operands += [queries[n], locals_[n]]
    state = pl.BlockSpec(before.shape, lambda i, s: (0, 0, 0))
    in_specs.append(state)
    operands.append(before)
    bit, out_specs, out_shape = None, [], []
    if last is not None:
        mine, bit, got = last
        in_specs += [pl.BlockSpec(memory_space=pltpu.SMEM), state]
        operands += [mine, got]
        out_specs, out_shape = [state], [jax.ShapeDtypeStruct(before.shape, jnp.float32)]
    in_specs += [pl.BlockSpec(memory_space=pl.ANY)] * len(tokens)
    more = EXTRA if embed else 0
    return pl.pallas_call(
        functools.partial(late_kernel, count, heads, embed, bit),
        grid_spec=pltpu.PrefetchScalarGridSpec(
            num_scalar_prefetch=1,
            grid=(steps,),
            in_specs=in_specs,
            out_specs=[
                pl.BlockSpec((rows + (more if n == 0 else 0), span), lambda i, s: (i, 0)) for n in range(count)
            ] + out_specs,
        ),
        out_shape=[
            jax.ShapeDtypeStruct((size + (more if n == 0 else 0), span), jnp.bfloat16) for n in range(count)
        ] + out_shape,
        compiler_params=params(),
        cost_estimate=COST,
        name="late_rows",
    )(at, *operands, *tokens)


def early_out_kernel(*refs):
    ins, outs = refs[:-2], refs[-2:]
    for side in range(2):
        low_ref, high_ref, q_ref, b_ref = ins[side::2]
        out_ref = outs[side]
        parts = []
        for c in range(b_ref.shape[1] // DH):
            high = min((c + 1) * EXTRA, DH)
            parts.append(b_ref[pl.ds(b_ref.shape[0] - EXTRA, high - c * EXTRA), pl.ds(c * DH, DH)])
        state = jnp.concatenate(parts, axis=0)
        size, held, first = out_ref.shape[0], q_ref.shape[0], low_ref.shape[0]
        query = jnp.concatenate([q_ref[...], high_ref[pl.ds(size - first, size - held), :]], axis=0)
        late = jnp.dot(query, state, preferred_element_type=jnp.float32)
        low = low_ref[...].astype(jnp.float32) + late[:first]
        out_ref[pl.ds(0, first), :] = low.astype(jnp.bfloat16)
        high = high_ref[pl.ds(0, size - first), :].astype(jnp.float32) + late[first:]
        out_ref[pl.ds(first, size - first), :] = high.astype(jnp.bfloat16)


def early_out(size, low, high, query, states):
    def full(array):
        return pl.BlockSpec(array.shape, lambda n: (0, 0))

    out = jax.ShapeDtypeStruct((size, DH), jnp.bfloat16)
    operands = [*low, *high, *query, *states]
    return pl.pallas_call(
        early_out_kernel,
        grid=(1,),
        in_specs=[full(y) for y in operands],
        out_specs=[pl.BlockSpec((size, DH), lambda n: (0, 0))] * 2,
        out_shape=[out, out],
        compiler_params=params(),
        cost_estimate=COST,
        name="early_out",
    )(*operands)


def gather_kernel(own_ref, mate_ref, o2_ref, o3_ref, out_ref):
    first = 0
    for ref in (own_ref, mate_ref, o2_ref, o3_ref):
        out_ref[:, pl.ds(first, ref.shape[1])] = ref[...]
        first += ref.shape[1]


def gather_rows(size, *pairs):
    def at(pair):
        index = pair[1] // size
        return pl.BlockSpec((size, pair[0].shape[1]), lambda n: (index, 0))

    width = sum(pair[0].shape[1] for pair in pairs)
    return pl.pallas_call(
        gather_kernel,
        grid=(1,),
        in_specs=[at(pair) for pair in pairs],
        out_specs=pl.BlockSpec((size, width), lambda n: (0, 0)),
        out_shape=jax.ShapeDtypeStruct((size, width), jnp.bfloat16),
        compiler_params=params(),
        cost_estimate=COST,
        name="gather_rows",
    )(*[pair[0] for pair in pairs])


def norm_last(head, gain, share, row, near, x2, x3, out):
    size, narrow = x2.shape
    width = narrow + DH
    index = row // size
    vmem = pl.BlockSpec(memory_space=pltpu.VMEM)

    def kernel(head_ref, gain_ref, near_ref, x2_ref, x3_ref, old_ref, out_ref):
        cut = [0, width, 2 * width, 2 * width + DH, 2 * width + 2 * DH]
        refs = [near_ref.at[:, pl.ds(a, b - a)] for a, b in zip(cut, cut[1:])]
        norm_kernel(head_ref, gain_ref, refs[0], refs[1], x2_ref, x3_ref, refs[2], refs[3], out_ref)

    return pl.pallas_call(
        kernel,
        grid_spec=pltpu.PrefetchScalarGridSpec(
            num_scalar_prefetch=1,
            grid=(1,),
            in_specs=[vmem] * 4 + [pl.BlockSpec(memory_space=pl.ANY)],
            out_specs=pl.BlockSpec((size, 4 * width), lambda n, s: (index, 0)),
        ),
        out_shape=jax.ShapeDtypeStruct((share, 4 * width), jnp.bfloat16),
        input_output_aliases={5: 0},
        compiler_params=params(),
        cost_estimate=COST,
        name="norm_last",
    )(head, gain, near, x2, x3, out)


def norm_kernel(head_ref, gain_ref, own_ref, mate_ref, x2_ref, x3_ref, o2_ref, o3_ref, *rest):
    out_ref = rest[-1]
    head = head_ref[0]
    width = own_ref.shape[1]
    pieces = (
        (own_ref, 0, 0), (mate_ref, 1, 0), (x2_ref, 2, 0), (o2_ref, 2, width - DH), (x3_ref, 3, 0),
        (o3_ref, 3, width - DH),
    )
    total = jnp.zeros((own_ref.shape[0], DH), jnp.float32)
    for ref, _, _ in pieces:
        for c in range(ref.shape[1] // DH):
            wide = ref[:, pl.ds(c * DH, DH)].astype(jnp.float32)
            total += wide * wide
    total = jnp.sum(total, axis=-1, keepdims=True)
    scale = lax.rsqrt(total / (4 * width) + EPS)
    for ref, partner, offset in pieces:
        at = pl.multiple_of((head ^ partner) * width + offset, DH)
        cols = pl.ds(at, ref.shape[1])
        out_ref[:, cols] = (ref[...].astype(jnp.float32) * scale * gain_ref[:, cols]).astype(jnp.bfloat16)


def norm_rows(head, gain, share, row, size, own, mate, x2, x3, o2, o3, out):
    def at(pair, cols):
        index = pair[1] // TILE
        return pl.BlockSpec((TILE, cols), lambda n, s: (index + n, 0))

    width = own[0].shape[1]
    in_specs = [pl.BlockSpec(gain.shape, lambda n, s: (0, 0)), at(own, width), at(mate, width)]
    in_specs += [at(x2, width - DH), at(x3, width - DH), at(o2, DH), at(o3, DH)]
    operands = [gain, own[0], mate[0], x2[0], x3[0], o2[0], o3[0]]
    aliases = {}
    if out is not None:
        in_specs.append(pl.BlockSpec(memory_space=pl.ANY))
        operands.append(out)
        aliases = {len(operands): 0}
    index = row // TILE
    return pl.pallas_call(
        norm_kernel,
        grid_spec=pltpu.PrefetchScalarGridSpec(
            num_scalar_prefetch=1,
            grid=(size // TILE,),
            in_specs=in_specs,
            out_specs=pl.BlockSpec((TILE, 4 * width), lambda n, s: (index + n, 0)),
        ),
        out_shape=jax.ShapeDtypeStruct((share, 4 * width), jnp.bfloat16),
        input_output_aliases=aliases,
        compiler_params=params(),
        cost_estimate=COST,
        name="norm_rows",
    )(head, *operands)


def norm_block_kernel(row, size, places, width, head_ref, *refs):
    count, tiles = len(places), size // TILE
    ins = refs[:count + 1]
    out_ref, gain_buf, *bufs, out_buf, gain_sem, in_sem, out_sem = refs[len(refs) - count - 6:]
    gain_copy = pltpu.make_async_copy(ins[0], gain_buf, gain_sem)
    gain_copy.start()
    copies = []
    for t in range(tiles):
        here = pl.ds(t * TILE, TILE)
        copies.append([])
        for n in range(count):
            there = pl.ds(places[n][0] + t * TILE, TILE)
            copy = pltpu.make_async_copy(ins[n + 1].at[there], bufs[n].at[here], in_sem.at[t, n])
            copy.start()
            copies[t].append(copy)
    gain_copy.wait()
    head = head_ref[0]
    sent = []
    for t in range(tiles):
        here = pl.ds(t * TILE, TILE)
        for copy in copies[t]:
            copy.wait()
        total = jnp.zeros((TILE, DH), jnp.float32)
        for buf in bufs:
            for c in range(buf.shape[1] // DH):
                wide = buf[here, pl.ds(c * DH, DH)].astype(jnp.float32)
                total += wide * wide
        scale = lax.rsqrt(jnp.sum(total, axis=-1, keepdims=True) / (4 * width) + EPS)
        for buf, (_, partner, offset) in zip(bufs, places):
            at = pl.multiple_of((head ^ partner) * width + offset, DH)
            cols = pl.ds(at, buf.shape[1])
            out_buf[here, cols] = (buf[here, :].astype(jnp.float32) * scale * gain_buf[:, cols]).astype(jnp.bfloat16)
        copy = pltpu.make_async_copy(out_buf.at[here], out_ref.at[pl.ds(row + t * TILE, TILE)], out_sem.at[t])
        copy.start()
        sent.append(copy)
    for copy in sent:
        copy.wait()


def norm_block(head, gain, share, row, size, own, mate, x2, x3, o2, o3, out):
    width = own[0].shape[1]
    pieces = ((own, 0, 0), (mate, 1, 0), (x2, 2, 0), (o2, 2, width - DH), (x3, 3, 0), (o3, 3, width - DH))
    arrays = [piece[0][0] for piece in pieces]
    places = [(piece[0][1], piece[1], piece[2]) for piece in pieces]
    anywhere = pl.BlockSpec(memory_space=pl.ANY)
    operands = [gain, *arrays] + ([] if out is None else [out])
    tiles = size // TILE
    return pl.pallas_call(
        functools.partial(norm_block_kernel, row, size, places, width),
        in_specs=[pl.BlockSpec(memory_space=pltpu.SMEM)] + [anywhere] * len(operands),
        out_specs=anywhere,
        out_shape=jax.ShapeDtypeStruct((share, 4 * width), jnp.bfloat16),
        input_output_aliases={} if out is None else {len(operands): 0},
        scratch_shapes=[pltpu.VMEM(gain.shape, jnp.float32)]
        + [pltpu.VMEM((size, array.shape[1]), jnp.bfloat16) for array in arrays]
        + [
            pltpu.VMEM((size, 4 * width), jnp.bfloat16),
            pltpu.SemaphoreType.DMA(()),
            pltpu.SemaphoreType.DMA((tiles, len(arrays))),
            pltpu.SemaphoreType.DMA((tiles,)),
        ],
        compiler_params=params(),
        cost_estimate=COST,
        name="norm_block",
    )(head, *operands)


def add_kernel(bit, with_before, mine_ref, total_ref, got_ref, *rest):
    group_ref, after_ref = rest[-2:]
    got = got_ref[...].astype(jnp.float32)
    late = jnp.where((mine_ref[0] & bit) > 0, got, 0.0)
    if with_before:
        late = late + rest[0][...]
    after_ref[...] = late
    group_ref[...] = (total_ref[...].astype(jnp.float32) + got).astype(jnp.bfloat16)


def add_step(mine, bit, total, got, before, tokens):
    vmem = pl.BlockSpec(memory_space=pltpu.VMEM)
    states = [total, got] + ([] if before is None else [before])
    return pl.pallas_call(
        functools.partial(add_kernel, bit, before is not None),
        in_specs=[pl.BlockSpec(memory_space=pltpu.SMEM)] + [vmem] * len(states)
        + [pl.BlockSpec(memory_space=pl.ANY)] * len(tokens),
        out_specs=[vmem, vmem],
        out_shape=[
            jax.ShapeDtypeStruct(total.shape, jnp.bfloat16),
            jax.ShapeDtypeStruct(total.shape, jnp.float32),
        ],
        compiler_params=params(),
        cost_estimate=COST,
        name="add_step",
    )(mine, *states, *tokens)


def swap(x, axis, size, bit):
    return lax.ppermute(x, axis, [(i, i ^ bit) for i in range(size)])


def across(pair):
    return [swap(x, "head", 4, k) for x, k in zip(pair, (2, 3))]


def shards(seq_size, queries, keys, values, norm_gain):
    rows, width = queries.shape
    heads = width // DH
    share = rows // 4
    head = lax.axis_index("head")
    at = jnp.full((1,), head, jnp.int32)
    mine = jnp.full((1,), lax.axis_index("seq"), jnp.int32)
    gain = norm_gain.reshape(1, -1)
    far = (2, 3)

    tail = HALF
    slices = [lax.dynamic_slice(queries, ((head ^ k) * share, width - DH), (share - tail, DH)) for k in far]
    early_q = across(slices)
    within, total = block_states(keys, values, *slices)
    arrays = (queries, keys, values, within)
    group, before, bit, step = total, None, 1, 0
    early_l = []
    while bit < seq_size:
        got = swap(group, "seq", seq_size, bit)
        tokens = []
        if step < 2:
            early = early_rows(at, queries, keys, values, within, step, tail * step, [group])
            early_l.append(across(early))
            tokens = [*early, *(early_q if step == 0 else early_l[0])]
        elif step == 2:
            first = attention_rows(
                arrays, None, at, far, BLK, HALF, 0, heads - 1, jnp.float32, [group], keep=True
            )
            second = attention_rows(arrays, None, at, far[:1], 0, BLK, 0, heads - 1, jnp.bfloat16, first)
            tokens = [*first, *second]
        if bit * 2 < seq_size:
            group, before = add_step(mine, bit, group, got, before, tokens)
        bit, step = bit * 2, step + 1

    def far_rows(start, size, tokens, cost=None, cut=1):
        return attention_rows(arrays, before, at, far, start, size, 0, heads - 1, jnp.bfloat16, tokens, cost, cut)

    *one, before = late_rows(
        at, first[2:], first[:2], before, heads - 1, True, [*early_l[1], *second], (mine, bit // 2, got)
    )
    x1 = across(one)
    two = late_rows(at, [(queries, far[0])], second, before, heads - 1, False, one, None)
    two += attention_rows(arrays, before, at, far[1:], 0, BLK, 0, heads - 1, jnp.bfloat16, two)
    x2 = across(two)
    mate = attention_quarter(arrays, before, at, 1, jnp.bfloat16, two)
    mated = swap(mate, "head", 4, 1)
    own = attention_quarter(arrays, before, at, 0, jnp.bfloat16, [mate])
    three = far_rows(BLK + HALF, HALF, [own, *x1], LONG, 2)
    x3, x4 = across(three[0::2]), across(three[1::2])
    state = lax.slice(x1[0], (HALF, 0), (HALF + EXTRA, x1[0].shape[1]))
    other = swap(state, "head", 4, 1)
    o2, o3 = early_out(share, *early_l, early_q, [state, other])
    out = None
    end = share - HALF // 2
    for row, size, (y2, y3) in ((BLK, HALF, x1), (0, BLK, x2), (BLK + HALF, HALF // 2, x3)):
        norm = norm_block if size == BLK else norm_rows
        out = norm(
            at, gain, share, row, size, (own, row), (mated, row), (y2, 0), (y3, 0), (o2, row), (o3, row), out
        )
    near = gather_rows(share - end, (own, end), (mated, end), (o2, end), (o3, end))
    return norm_last(at, gain, share, end, near, x4[0], x4[1], out)


def solution(mesh):
    seq_size = mesh.shape["seq"]

    def body(queries, keys, values, norm_gain):
        return shards(seq_size, queries, keys, values, norm_gain)

    return jax.shard_map(
        body,
        mesh=mesh,
        in_specs=(P("seq", "head"), P("seq", "head"), P("seq", "head"), P()),
        out_specs=P(("seq", "head"), None),
        check_vma=False,
    )
```
